512 devices in a mesh: cd: 32 (over z_hi, y, x), ab: 16 (over z_lo, core).
Axes of the slice: x: 4, y: 4, z: 16 (z_hi: 2, z_lo: 8; z = z_hi * 8 + z_lo), core: 2. Of those that a mesh axis runs over, the one named last changes fastest.
Arguments:
- amplitudes: float32 [384, 65536], P('ab', 'cd'), may hold values from -6 to 6
- integrals: float32 [65536, 8192], P('cd', 'ab'), may hold values from -0.046875 to 0.046875
- residual_in: float32 [384, 8192], P('cd', 'ab'), may hold values from -6 to 6
- pair_irrep_ij: int32 [384], P('ab'), may hold values from 0 to 3
- pair_irrep_cd: int32 [65536], P('cd'), may hold values from 0 to 3
- pair_irrep_ab: int32 [8192], P('ab'), may hold values from 0 to 3
Outputs:
- residual_out: float32 [384, 8192], P('cd', 'ab')
The draws below stay inside these ranges and needn't reach their ends.
All inputs are finite; a program needn't handle non-finite values.
Results may differ from the reference program's by a relative error of at most 0.0003.
Values sent between devices are 32-bit elements; how exact they have to be, the bound alone decides.
A program may use at most 64 MiB of HBM per device.

```python
import math
import jax
import jax.numpy as jnp
import numpy as np
from jax import lax

AB_DEV = 512
IRREPS = 4
IJ = 384
CD = 65536
AB = 8192
N_AB = 16


def plant(values, stream_key, least, high):
    dims = values.shape
    place = [jax.random.randint(jax.random.fold_in(stream_key, axis), (), 0, dims[axis]) for axis in range(len(dims))]
    values = values.at[tuple(place)].set(least)
    longest = dims.index(max(dims))
    place[longest] = (place[longest] + 1) % dims[longest]
    return values.at[tuple(place)].set(high)


def raised(array, key, source, target, blocks, factor):
    owner, partner = [(jnp.arange(array.shape[dim]) // (array.shape[dim] // blocks)).reshape([-1 if axis == dim else 1 for axis in range(array.ndim)]) for dim in (source, target)]
    chosen = jax.random.permutation(key, blocks)[partner]
    strong = (owner == chosen) | (owner == (partner + blocks // 2) % blocks)
    return jnp.where(strong, factor * array, array)


def block_levels(own_key, extent, pieces, least, top_value):
    def one(dim, blocks):
        draws = jax.random.uniform(jax.random.fold_in(jax.random.fold_in(own_key, 6), dim), (blocks,), jnp.float32, least / len(pieces), top_value / len(pieces))
        return jnp.repeat(jnp.exp(draws), extent[dim] // blocks).reshape((-1,) + (1,) * (len(extent) - dim - 1))

    level = one(*pieces[0])
    for cut in pieces[1:]:
        level = level * one(*cut)
    return level


def rank_table(amount, skew):
    portions = [(1 << 20) // math.isqrt(standing ** skew) + 1 for standing in range(1, amount + 1)]
    scale = 1 + sum(portions) // (1 << 30)
    return np.cumsum(np.array([max(1, weight // scale) for weight in portions]))


def ranked(stream_key, extent, count, lean):
    table = rank_table(count, lean)
    pick = jax.random.randint(jax.random.fold_in(stream_key, 1), extent, 0, int(table[count - 1]))
    rank = jnp.searchsorted(jnp.asarray(table, jnp.int32), pick, side="right")
    return jax.random.permutation(jax.random.fold_in(stream_key, 2), count)[rank].astype(jnp.int32)


def centred(stream_key, shape, scale, reach, pieces=(), held_as=jnp.bfloat16):
    gain = block_levels(stream_key, shape, pieces, -0.22, 0.18) if pieces else 1.0
    array = jax.random.normal(stream_key, shape, jnp.float32) * scale * gain
    return jnp.minimum(jnp.maximum(array, -reach), reach).astype(held_as)


def heavy_noise(key, extent, scale, bound, shards, heavy, kind=jnp.bfloat16):
    values = scale * jax.random.normal(key, extent, jnp.float32)
    if shards:
        values = values * block_levels(key, extent, shards, -0.22, 0.18)
    return jnp.clip(raised(values, jax.random.fold_in(key, 3), *heavy), -bound, bound).astype(kind)


def setup_inputs(seed: int = 0) -> dict:
    key_list = jax.random.split(jax.random.key(seed), 7)
    amplitudes = heavy_noise(key_list[0], (IJ, CD), 1.0, 6.0, ((0, 16), (1, 32)), (1, 0, 32, 2.75), jnp.float32)
    integrals = centred(key_list[1], (CD, AB), (CD // 4) ** -0.5, 0.046875, ((0, 32), (1, 16)), jnp.float32)
    residual_in = centred(key_list[2], (IJ, AB), 1.0, 6.0, ((0, 32), (1, 16)), jnp.float32)
    pair_irrep_ij = plant(ranked(key_list[3], (IJ,), IRREPS, 2), jax.random.fold_in(key_list[3], 3), 0, IRREPS - 1).astype(jnp.int32)
    pair_irrep_cd = plant(ranked(key_list[4], (CD,), IRREPS, 2), jax.random.fold_in(key_list[4], 3), 0, IRREPS - 1).astype(jnp.int32)
    pair_irrep_ab = plant(ranked(key_list[5], (AB,), IRREPS, 2), jax.random.fold_in(key_list[5], 3), 0, IRREPS - 1).astype(jnp.int32)
    return {"amplitudes": amplitudes, "integrals": integrals, "residual_in": residual_in, "pair_irrep_ij": pair_irrep_ij, "pair_irrep_cd": pair_irrep_cd, "pair_irrep_ab": pair_irrep_ab}


def reference(amplitudes, integrals, residual_in, pair_irrep_ij, pair_irrep_cd, pair_irrep_ab):
    masked_t2 = jnp.where(pair_irrep_ij[:, None] == pair_irrep_cd[None, :], amplitudes, jnp.zeros_like(amplitudes))

    def column_block(index):
        start = (index * AB_DEV).astype(jnp.int32)
        block = lax.dynamic_slice_in_dim(integrals, start, AB_DEV, 1)
        labels = lax.dynamic_slice_in_dim(pair_irrep_ab, start, AB_DEV, 0)
        masked_v = jnp.where(pair_irrep_cd[:, None] == labels[None, :], block, jnp.zeros_like(block))
        return jnp.dot(masked_t2, masked_v, precision=lax.Precision.HIGHEST, preferred_element_type=jnp.float32)

    blocks = lax.map(column_block, jnp.arange(N_AB, dtype=jnp.int32))
    product = jnp.transpose(blocks, (1, 0, 2)).reshape(IJ, AB)
    return residual_in + product
```

```python
import functools

import jax
import jax.numpy as jnp
from jax import lax
from jax.experimental import pallas as pl
from jax.experimental.pallas import tpu as pltpu
from jax.sharding import PartitionSpec as P

MESH = pl.DeviceIdType.MESH
CORES = 2
NX = 4
SUB = 8


def kernel(line, ny, nz, t_hbm, v_hbm, ij_ref, cd_ref, ab_ref, out_ref,
           tbuf, vraw, vhi, vlo, sbuf, xr, ys, yr, zs, zr, keep,
           t_sem, v_sem, line_recv, line_send, sib_recv, sib_send,
           x_recv, x_send, y_recv, y_send, z_recv, z_send):
    p, q = lax.axis_index("cd"), lax.axis_index("ab")
    x, y, h = p % NX, (p // NX) % ny, p // (NX * ny)
    core, i = q % CORES, q // CORES
    rows, depth = t_hbm.shape
    cols = v_hbm.shape[1]
    half = cols // 2
    subs = rows // SUB
    chunks = v_sem.shape[0]
    chunk = depth // chunks

    def plane(yy, xx):
        return (h * ny * NX + yy * NX + xx, q)

    sibling = (p, i * CORES + 1 - core)
    right, left = (p, q + CORES), (p, q - CORES)
    partner = ((p + ny * NX) % (nz * ny * NX), q)

    t_in = pltpu.make_async_copy(t_hbm, tbuf.at[q], t_sem)
    t_in.start()
    v_in = [pltpu.make_async_copy(v_hbm.at[pl.ds(c * chunk, chunk)], vraw.at[pl.ds(c * chunk, chunk)], v_sem.at[c])
            for c in range(chunks)]
    for copy in v_in:
        copy.start()

    barrier = pltpu.get_barrier_semaphore()

    def greet(device):
        pl.semaphore_signal(barrier, inc=1, device_id=device, device_id_type=MESH)

    greet(sibling)
    for d in range(1, NX):
        greet(plane(y, (x + d) % NX))
    for d in range(1, ny):
        greet(plane((y + d) % ny, x))
    if nz > 1:
        greet(partner)
    pl.when(i > 0)(lambda: greet(left))
    pl.when(i < line - 1)(lambda: greet(right))
    t_in.wait()

    sub = lax.broadcasted_iota(jnp.int32, (SUB, 128), 0)
    for g in range(subs):
        label = jnp.zeros((SUB, 128), jnp.int32)
        for r in range(SUB):
            label = jnp.where(sub == r, ij_ref[g * SUB + r], label)
        for c in range(0, depth, 128):
            block = tbuf[q, g * SUB:(g + 1) * SUB, c:c + 128]
            tbuf[q, g * SUB:(g + 1) * SUB, c:c + 128] = jnp.where(label == cd_ref[:, c:c + 128], block, 0.0)

    others = 1 + (NX - 1) + (ny - 1) + (1 if nz > 1 else 0)
    ends = jnp.where(i > 0, 1, 0) + jnp.where(i < line - 1, 1, 0)
    pl.semaphore_wait(barrier, others + ends)

    def line_copy(j, c, way, device):
        part = tbuf.at[j * CORES + core, pl.ds(c * SUB, SUB)]
        return pltpu.make_async_remote_copy(
            src_ref=part, dst_ref=part, send_sem=line_send.at[way, j, c], recv_sem=line_recv.at[j, c],
            device_id=device, device_id_type=MESH)

    def sib_copy(j, c):
        part = tbuf.at[j * CORES + core, pl.ds(c * SUB, SUB)]
        return pltpu.make_async_remote_copy(
            src_ref=part, dst_ref=part, send_sem=sib_send.at[j, c], recv_sem=sib_recv.at[j, c],
            device_id=sibling, device_id_type=MESH)

    def sib_wait(j, c):
        part = tbuf.at[j * CORES + 1 - core, pl.ds(c * SUB, SUB)]
        pltpu.make_async_remote_copy(
            src_ref=part, dst_ref=part, send_sem=sib_send.at[j, c], recv_sem=sib_recv.at[j, c],
            device_id=sibling, device_id_type=MESH).wait_recv()

    def forward(j, c, act):
        pl.when((j <= i) & (i < line - 1))(lambda: act(line_copy(j, c, 0, right)))
        pl.when((j >= i) & (i > 0))(lambda: act(line_copy(j, c, 1, left)))
        act(sib_copy(j, c))

    for c in range(subs):
        forward(i, c, lambda copy: copy.start())

    for c in range(chunks):
        v_in[c].wait()

        @pl.loop(0, chunk // 128)
        def _(b):
            start = pl.multiple_of(c * chunk + b * 128, 128)
            label = jnp.broadcast_to(cd_ref[:, pl.ds(start, 128)], (128, 128)).T
            for l in range(0, cols, 128):
                v = jnp.where(label == ab_ref[:, l:l + 128], vraw[pl.ds(start, 128), l:l + 128], 0.0)
                hi = v.astype(jnp.bfloat16)
                vhi[pl.ds(start, 128), l:l + 128] = hi
                vlo[pl.ds(start, 128), l:l + 128] = (v - hi.astype(jnp.float32)).astype(jnp.bfloat16)

    def x_copy(j, k, device):
        return pltpu.make_async_remote_copy(
            src_ref=sbuf.at[j, k], dst_ref=xr.at[j, x], send_sem=x_send.at[j, k], recv_sem=x_recv.at[j, x],
            device_id=device, device_id_type=MESH)

    def x_wait(j, k):
        pltpu.make_async_remote_copy(
            src_ref=sbuf.at[j, k], dst_ref=xr.at[j, k], send_sem=x_send.at[j, k], recv_sem=x_recv.at[j, k],
            device_id=plane(y, k), device_id_type=MESH).wait_recv()

    def y_copy(j):
        return pltpu.make_async_remote_copy(
            src_ref=ys.at[j], dst_ref=yr.at[j // ny, y], send_sem=y_send.at[j], recv_sem=y_recv.at[j // ny, y],
            device_id=plane(j % ny, x), device_id_type=MESH)

    def y_wait(hh, yy):
        pltpu.make_async_remote_copy(
            src_ref=ys.at[0], dst_ref=yr.at[hh, yy], send_sem=y_send.at[0], recv_sem=y_recv.at[hh, yy],
            device_id=plane(yy, x), device_id_type=MESH).wait_recv()

    def z_copy():
        return pltpu.make_async_remote_copy(
            src_ref=zs, dst_ref=zr, send_sem=z_send, recv_sem=z_recv, device_id=partner, device_id_type=MESH)

    low = lax.broadcasted_iota(jnp.int32, (8, half), 0) < 4

    def multiply(j):
        t = tbuf[pl.ds(j * CORES, CORES)].reshape(CORES * rows, depth)
        hi = t.astype(jnp.bfloat16)
        lo = (t - hi.astype(jnp.float32)).astype(jnp.bfloat16)
        a = jnp.dot(jnp.concatenate([hi, lo], axis=0), vhi[...], preferred_element_type=jnp.float32)
        b = jnp.dot(hi, vlo[...], preferred_element_type=jnp.float32)
        total = a[:CORES * rows] + a[CORES * rows:] + b
        for k in range(NX):
            base = (k // 2) * rows
            middle = total[base + 8:base + 16]
            turned = pltpu.roll(middle, 4, 0)
            if k % 2 == 0:
                full = total[base:base + 8]
                rest = jnp.where(low, middle[:, :half], turned[:, half:])
            else:
                full = total[base + 16:base + 24]
                rest = jnp.where(low, turned[:, :half], middle[:, half:])
            sbuf[j, k, :, :cols] = full
            sbuf[j, k, :, cols:] = rest
        for d in range(1, NX):
            k = (x + d) % NX
            x_copy(j, k, plane(y, k)).start()

    def reduce_x(j):
        for d in range(1, NX):
            x_wait(j, (x + d) % NX)
        mine = sbuf[j, x]
        for d in range(1, NX):
            mine = mine + xr[j, (x + d) % NX]
        ys[j] = mine
        pl.when(j % ny != y)(lambda: y_copy(j).start())

    def reduce_y(j):
        @pl.when(j % ny == y)
        def _():
            hh = j // ny
            for d in range(1, ny):
                y_wait(hh, (y + d) % ny)
            mine = ys[j]
            for d in range(1, ny):
                mine = mine + yr[hh, (y + d) % ny]

            @pl.when(hh == h)
            def _():
                keep[...] = mine

            @pl.when(hh != h)
            def _():
                zs[...] = mine
                z_copy().start()

    def let_go(j):
        for c in range(subs):
            forward(j, c, lambda copy: copy.wait_send())
        for d in range(1, NX):
            k = (x + d) % NX
            x_copy(j, k, plane(y, k)).wait_send()
        pl.when(j % ny != y)(lambda: y_copy(j).wait_send())

    def at(step, act):
        @pl.loop(0, 2)
        def _(side):
            j = i - step + side * 2 * step
            pl.when((j >= 0) & (j < line) & (step + 1 - side > 0))(lambda: act(j))

    @pl.loop(0, line + 2)
    def _(step):
        @pl.when(step < line)
        def _():
            @pl.when(step > 0)
            def _():
                @pl.loop(0, subs)
                def _(c):
                    def take(j):
                        line_copy(j, c, 0, right).wait_recv()
                        forward(j, c, lambda copy: copy.start())

                    pl.when(i - step >= 0)(lambda: take(i - step))
                    pl.when(i + step < line)(lambda: take(i + step))

            def ready(j):
                for c in range(subs):
                    sib_wait(j, c)
                multiply(j)

            at(step, ready)

        pl.when((step >= 1) & (step <= line))(lambda: at(step - 1, reduce_x))
        pl.when(step >= 2)(lambda: at(step - 2, reduce_y))

    if nz > 1:
        z_copy().wait_recv()
    mine = keep[...]
    if nz > 1:
        mine = mine + zr[...]
    full, rest = mine[:, :cols], mine[:, cols:]
    turned = pltpu.roll(rest, 4, 0)

    @pl.when(x % 2 == 0)
    def _():
        out_ref[:8] = full
        out_ref[8:12, :half] = rest[:4]
        out_ref[8:12, half:] = turned[:4]

    @pl.when(x % 2 == 1)
    def _():
        out_ref[:4, :half] = rest[:4]
        out_ref[:4, half:] = turned[:4]
        out_ref[4:12] = full

    @pl.loop(0, line)
    def _(j):
        let_go(j)
    if nz > 1:
        z_copy().wait_send()


def ladder(line, ny, nz, amplitudes, integrals, ij, cd, ab):
    rows, depth = amplitudes.shape
    cols = integrals.shape[1]
    subs = rows // SUB
    piece = (8, cols + cols // 2)
    dma = pltpu.SemaphoreType.DMA
    vmem = pl.BlockSpec(memory_space=pltpu.VMEM)
    chunks = min(4, depth // 128)
    return pl.pallas_call(
        functools.partial(kernel, line, ny, nz),
        out_shape=jax.ShapeDtypeStruct((rows // 2, cols), jnp.float32),
        in_specs=[pl.BlockSpec(memory_space=pltpu.HBM), pl.BlockSpec(memory_space=pltpu.HBM),
                  pl.BlockSpec(memory_space=pltpu.SMEM), vmem, vmem],
        out_specs=vmem,
        scratch_shapes=[
            pltpu.VMEM((line * CORES, rows, depth), jnp.float32),
            pltpu.VMEM((depth, cols), jnp.float32),
            pltpu.VMEM((depth, cols), jnp.bfloat16),
            pltpu.VMEM((depth, cols), jnp.bfloat16),
            pltpu.VMEM((line, NX) + piece, jnp.float32),
            pltpu.VMEM((line, NX) + piece, jnp.float32),
            pltpu.VMEM((line,) + piece, jnp.float32),
            pltpu.VMEM((nz, ny) + piece, jnp.float32),
            pltpu.VMEM(piece, jnp.float32),
            pltpu.VMEM(piece, jnp.float32),
            pltpu.VMEM(piece, jnp.float32),
            dma, dma((chunks,)),
            dma((line, subs)), dma((2, line, subs)),
            dma((line, subs)), dma((line, subs)),
            dma((line, NX)), dma((line, NX)),
            dma((nz, ny)), dma((line,)),
            dma, dma,
        ],
        compiler_params=pltpu.CompilerParams(
            collective_id=0, has_side_effects=True, vmem_limit_bytes=48 * 1024 * 1024),
    )(amplitudes, integrals, ij, cd.reshape(1, depth), ab.reshape(1, cols))


def solution(mesh):
    line = mesh.shape["ab"] // CORES
    planes = mesh.shape["cd"] // NX
    ny = min(4, planes)
    nz = planes // ny

    def body(amplitudes, integrals, residual_in, ij, cd, ab):
        return residual_in + ladder(line, ny, nz, amplitudes, integrals, ij, cd, ab)

    placed = (P("ab", "cd"), P("cd", "ab"), P("cd", "ab"), P("ab"), P("cd"), P("ab"))
    return jax.shard_map(body, mesh=mesh, in_specs=placed, out_specs=P("cd", "ab"), check_vma=False)
```

```python
import functools

import jax
import jax.numpy as jnp
from jax import lax
from jax.experimental import pallas as pl
from jax.experimental.pallas import tpu as pltpu
from jax.sharding import PartitionSpec as P

MESH = pl.DeviceIdType.MESH
CORES = 2
NX = 4
NY = 4
SUB = 8
CUTS = 2
PARTS = 4
FIRST = 4


def kernel(line, ny, nz, t_hbm, v_hbm, res_hbm, ij_hbm, cd_hbm, ab_hbm, out_ref,
           tbuf, vraw, vhi, vlo, acc, sbuf, xr, ys, yr, zs, zr, keep, res, ij_ref, cd_ref, ab_ref,
           t_sem, v_sem, small_sem, line_recv, line_send, sib_recv, sib_send,
           x_recv, x_send, y_recv, y_send, z_recv, z_send, z_here):
    p, q = lax.axis_index("cd"), lax.axis_index("ab")
    x, y, h = p % NX, (p // NX) % ny, p // (NX * ny)
    core, i = q % CORES, q // CORES
    rows, depth = t_hbm.shape
    cols = v_hbm.shape[1]
    half = cols // 2
    subs = rows // SUB * CUTS
    width = depth // CUTS
    chunks = v_sem.shape[0]
    chunk = depth // chunks

    def plane(yy, xx):
        return (h * ny * NX + yy * NX + xx, q)

    sibling = (p, i * CORES + 1 - core)
    right, left = (p, q + CORES), (p, q - CORES)
    partner = ((p + ny * NX) % (nz * ny * NX), q)

    t_in = pltpu.make_async_copy(t_hbm, tbuf.at[q], t_sem)
    t_in.start()

    barrier = pltpu.get_barrier_semaphore()

    def greet(device):
        pl.semaphore_signal(barrier, inc=1, device_id=device, device_id_type=MESH)

    if nz > 1:
        pl.when(h == 0)(lambda: greet(partner))
    pl.when(i > 0)(lambda: greet(left))
    pl.when(i < line - 1)(lambda: greet(right))
    for d in range(1, NX):
        greet(plane(y, (x + d) % NX))
    for d in range(1, ny):
        greet(plane((y + d) % ny, x))
    greet(sibling)

    small = [pltpu.make_async_copy(a, b, small_sem.at[n])
             for n, (a, b) in enumerate(((ij_hbm, ij_ref), (cd_hbm, cd_ref), (ab_hbm, ab_ref), (res_hbm, res)))]
    for copy in small:
        copy.start()
    v_in = [pltpu.make_async_copy(v_hbm.at[pl.ds(c * chunk, chunk)], vraw.at[pl.ds(c * chunk, chunk)], v_sem.at[c])
            for c in range(chunks)]
    for copy in v_in:
        copy.start()

    small[0].wait()
    small[1].wait()
    t_in.wait()
    sub = lax.broadcasted_iota(jnp.int32, (SUB, 128), 0)
    for g in range(rows // SUB):
        label = jnp.zeros((SUB, 128), jnp.int32)
        for r in range(SUB):
            label = jnp.where(sub == r, ij_ref[g * SUB + r], label)
        for c in range(0, depth, 128):
            block = tbuf[q, g * SUB:(g + 1) * SUB, c:c + 128]
            tbuf[q, g * SUB:(g + 1) * SUB, c:c + 128] = jnp.where(label == cd_ref[:, c:c + 128], block, 0.0)

    others = 1 + (NX - 1) + (ny - 1) + (jnp.where(h > 0, 1, 0) if nz > 1 else 0)
    ends = jnp.where(i > 0, 1, 0) + jnp.where(i < line - 1, 1, 0)
    pl.semaphore_wait(barrier, others + ends)

    def remote(src, dst, send, recv, device):
        return pltpu.make_async_remote_copy(
            src_ref=src, dst_ref=dst, send_sem=send, recv_sem=recv, device_id=device, device_id_type=MESH)

    def piece(j, which, c):
        start = pl.multiple_of(c % CUTS * width, width)
        return tbuf.at[j * CORES + which, pl.ds(pl.multiple_of(c // CUTS * SUB, SUB), SUB), pl.ds(start, width)]

    m = line // 2

    def behind(side):
        return jnp.where(side == 0, i, line - 1 - i)

    def number(side, b):
        return jnp.where(side == 0, b, line - 1 - b)

    def late(side):
        return (h == 1 - side) if nz > 1 else h < 0

    def near(side):
        return jnp.where(late(side), jnp.maximum(behind(side) - m, 0), 0)

    def arrival(side, n):
        k = near(side)
        r = n - k * FIRST
        t = r - m * subs
        rest = subs - FIRST
        b = jnp.where(k == 0, behind(side) - 1 - n // subs, m - 1 - r // subs)
        c = jnp.where(k == 0, n % subs, r % subs)
        before, after = (k > 0) & (r < 0), (k > 0) & (t >= 0)
        b = jnp.where(before, behind(side) - 1 - n // FIRST, jnp.where(after, m + t // rest, b))
        c = jnp.where(before, n % FIRST, jnp.where(after, FIRST + t % rest, c))
        return number(side, b), c

    def withheld(side):
        return late(side) & (behind(side) >= m) & (behind(side) < line - 1)

    def line_copy(j, c, way):
        part = piece(j, core, c)
        return remote(part, part, line_send.at[way, j], line_recv.at[j, c], right if way == 0 else left)

    def sib_copy(j, c):
        part = piece(j, core, c)
        return remote(part, part, sib_send.at[j], sib_recv.at[j], sibling)

    def forward(j, c, way):
        pl.when(i < line - 1 if way == 0 else i > 0)(lambda: line_copy(j, c, way).start())

    def forward_done(j):
        mine = tbuf.at[j * CORES + core]
        for way, there in ((0, (j <= i) & (i < line - 1)), (1, (j >= i) & (i > 0))):
            @pl.when(there & ((j != i) | jnp.logical_not(withheld(way))))
            def _():
                remote(mine, mine, line_send.at[way, j], line_recv.at[j, 0], sibling).wait_send()
        remote(mine, mine, sib_send.at[j], sib_recv.at[j], sibling).wait_send()

    def sib_wait(j):
        other = tbuf.at[j * CORES + 1 - core]
        remote(other, other, sib_send.at[j], sib_recv.at[j], sibling).wait_recv()

    for c in range(subs):
        for way in range(2):
            if c < FIRST:
                forward(i, c, way)
            else:
                pl.when(jnp.logical_not(withheld(way)))(lambda: forward(i, c, way))
    for c in range(subs):
        sib_copy(i, c).start()

    if nz > 1:
        @pl.when(h > 0)
        def _():
            pl.semaphore_signal(z_here, inc=1, device_id=partner, device_id_type=MESH)

    small[2].wait()
    for c in range(chunks):
        v_in[c].wait()

        @pl.loop(0, chunk // 128)
        def _(b):
            start = pl.multiple_of(c * chunk + b * 128, 128)
            label = jnp.broadcast_to(cd_ref[:, pl.ds(start, 128)], (128, 128)).T
            for l in range(0, cols, 128):
                v = jnp.where(label == ab_ref[:, l:l + 128], vraw[pl.ds(start, 128), l:l + 128], 0.0)
                hi = v.astype(jnp.bfloat16)
                vhi[pl.ds(start, 128), l:l + 128] = hi
                vlo[pl.ds(start, 128), l:l + 128] = (v - hi.astype(jnp.float32)).astype(jnp.bfloat16)

    def x_copy(j, d):
        k = (x + d) % NX
        return remote(sbuf.at[j, k], xr.at[j, d - 1], x_send.at[j], x_recv.at[j], plane(y, k))

    def y_copy(j):
        d = (j - y + ny) % ny
        return remote(ys.at[j], yr.at[j // ny, d - 1], y_send.at[j], y_recv.at[j // ny], plane(j % ny, x))

    def z_copy():
        return remote(zs, zr, z_send, z_recv, partner)

    low = lax.broadcasted_iota(jnp.int32, (8, half), 0) < 4

    def product(blocks, start, size):
        t = jnp.concatenate([tbuf[pl.ds(j * CORES, CORES), :, pl.ds(start, size)].reshape(CORES * rows, size)
                             for j in blocks], axis=0)
        n = t.shape[0]
        hi = t.astype(jnp.bfloat16)
        lo = (t - hi.astype(jnp.float32)).astype(jnp.bfloat16)
        a = jnp.dot(jnp.concatenate([hi, lo], axis=0), vhi[pl.ds(start, size)], preferred_element_type=jnp.float32)
        b = jnp.dot(hi, vlo[pl.ds(start, size)], preferred_element_type=jnp.float32)
        return a[:n] + a[n:] + b

    def hand_out(j, n):
        for k in range(NX):
            base = (k // 2) * rows
            middle = acc[n, base + 8:base + 16]
            turned = pltpu.roll(middle, 4, 0)
            if k % 2 == 0:
                full = acc[n, base:base + 8]
                rest = jnp.where(low, middle[:, :half], turned[:, half:])
            else:
                full = acc[n, base + 16:base + 24]
                rest = jnp.where(low, turned[:, :half], middle[:, half:])
            sbuf[j, k, :, :cols] = full
            sbuf[j, k, :, cols:] = rest
        for d in range(1, NX):
            x_copy(j, d).start()

    def reduce_x(j):
        remote(xr.at[j], xr.at[j], x_send.at[j], x_recv.at[j], sibling).wait_recv()
        mine = sbuf[j, x]
        for d in range(1, NX):
            mine = mine + xr[j, d - 1]
        ys[j] = mine
        pl.when(j % ny != y)(lambda: y_copy(j).start())

    def reduce_y(j):
        @pl.when(j % ny == y)
        def _():
            hh = j // ny
            mine = ys[j]
            if ny > 1:
                remote(yr.at[hh], yr.at[hh], y_send.at[j], y_recv.at[hh], sibling).wait_recv()
                for d in range(1, ny):
                    mine = mine + yr[hh, d - 1]

            @pl.when(hh == h)
            def _():
                keep[...] = mine

            @pl.when(hh != h)
            def _():
                zs[...] = mine
                pl.when(h == 0)(lambda: pl.semaphore_wait(z_here, 1))
                z_copy().start()

    def let_go(j):
        forward_done(j)
        sent = sbuf.at[j, pl.ds(0, NX - 1)]
        remote(sent, sent, x_send.at[j], x_recv.at[j], sibling).wait_send()
        pl.when(j % ny != y)(lambda: y_copy(j).wait_send())

    def complete(side, step):
        u, k = behind(side), near(side)
        b = jnp.where(k > 0, m + (k * FIRST + subs - 1) // subs, u) - step
        there = jnp.where(step == 0, side == 0, (step > 0) & (b >= 0) & (b < jnp.where(k > 0, m, u)))
        return there, jnp.where(step == 0, i, number(side, b))

    def rest(side, step, act):
        @pl.when(step == behind(side))
        def _():
            @pl.loop(0, near(side))
            def _(n):
                act(number(side, m + n))

    def at(step, act):
        @pl.loop(0, 2)
        def _(side):
            there, j = complete(side, step)
            pl.when(there)(lambda: act(j))
            rest(side, step, act)

    def whole(j):
        sib_wait(j)
        acc[0] = product([j], 0, depth)
        hand_out(j, 0)

    def both(step, part):
        (there, j), (there_too, j_too) = complete(0, step), complete(1, step)

        @pl.when(there | there_too)
        def _():
            @pl.when(part == 0)
            def _():
                pl.when(there)(lambda: sib_wait(j))
                pl.when(there_too)(lambda: sib_wait(j_too))

            size = depth // PARTS
            start = pl.multiple_of(part * size, size)
            term = product([jnp.where(there, j, j_too), jnp.where(there_too, j_too, j)], start, size)
            term = term.reshape(2, CORES * rows, cols)

            @pl.when(part == 0)
            def _():
                acc[...] = term

            @pl.when(part > 0)
            def _():
                acc[...] += term

            @pl.when(part == PARTS - 1)
            def _():
                pl.when(there)(lambda: hand_out(j, 0))
                pl.when(there_too)(lambda: hand_out(j_too, 1))

        @pl.when(part == PARTS - 1)
        def _():
            @pl.loop(0, 2)
            def _(side):
                rest(side, step, whole)

    end = (i == 0) | (i == line - 1)

    @pl.loop(0, line + 2)
    def _(step):
        @pl.loop(0, subs)
        def _(c):
            for side in range(2):
                @pl.when((step > 0) & (step <= behind(side)))
                def _():
                    j, piece_number = arrival(side, (step - 1) * subs + c)
                    line_copy(j, piece_number, side).wait_recv()
                    forward(j, piece_number, side)
                    sib_copy(j, piece_number).start()

            @pl.when(jnp.logical_not(end) & (c < PARTS))
            def _():
                both(step - 1, c)

        for side in range(2):
            @pl.when(withheld(side) & (step == behind(side)))
            def _():
                for c in range(FIRST, subs):
                    forward(i, c, side)

        pl.when(end)(lambda: at(step, whole))

        done = jnp.where(end, step, step - 1)
        at(done - 1, reduce_x)
        at(done - 2, reduce_y)
        at(done - 2, let_go)

    small[3].wait()
    if nz > 1:
        z_copy().wait_recv()
    mine = keep[...]
    if nz > 1:
        mine = mine + zr[...]
    full, rest = mine[:, :cols], mine[:, cols:]
    turned = pltpu.roll(rest, 4, 0)

    @pl.when(x % 2 == 0)
    def _():
        out_ref[:8] = full + res[:8]
        out_ref[8:12, :half] = rest[:4] + res[8:12, :half]
        out_ref[8:12, half:] = turned[:4] + res[8:12, half:]

    @pl.when(x % 2 == 1)
    def _():
        out_ref[:4, :half] = rest[:4] + res[:4, :half]
        out_ref[:4, half:] = turned[:4] + res[:4, half:]
        out_ref[4:12] = full + res[4:12]

    if nz > 1:
        z_copy().wait_send()
    for way in range(2):
        @pl.when(withheld(way))
        def _():
            mine = tbuf.at[i * CORES + core]
            remote(mine, mine, line_send.at[way, i], line_recv.at[i, 0], sibling).wait_send()


def ladder(line, ny, nz, amplitudes, integrals, residual, ij, cd, ab):
    rows, depth = amplitudes.shape
    cols = integrals.shape[1]
    subs = rows // SUB * CUTS
    piece = (8, cols + cols // 2)
    dma = pltpu.SemaphoreType.DMA
    chunks = min(4, depth // 128)
    return pl.pallas_call(
        functools.partial(kernel, line, ny, nz),
        out_shape=jax.ShapeDtypeStruct((rows // 2, cols), jnp.float32),
        in_specs=[pl.BlockSpec(memory_space=pltpu.HBM)] * 6,
        out_specs=pl.BlockSpec(memory_space=pltpu.VMEM),
        scratch_shapes=[
            pltpu.VMEM((line * CORES, rows, depth), jnp.float32),
            pltpu.VMEM((depth, cols), jnp.float32),
            pltpu.VMEM((depth, cols), jnp.bfloat16),
            pltpu.VMEM((depth, cols), jnp.bfloat16),
            pltpu.VMEM((2, CORES * rows, cols), jnp.float32),
            pltpu.VMEM((line, NX) + piece, jnp.float32),
            pltpu.VMEM((line, NX - 1) + piece, jnp.float32),
            pltpu.VMEM((line,) + piece, jnp.float32),
            pltpu.VMEM((nz, max(1, ny - 1)) + piece, jnp.float32),
            pltpu.VMEM(piece, jnp.float32),
            pltpu.VMEM(piece, jnp.float32),
            pltpu.VMEM(piece, jnp.float32),
            pltpu.VMEM((rows // 2, cols), jnp.float32),
            pltpu.SMEM((rows,), jnp.int32),
            pltpu.VMEM((1, depth), jnp.int32),
            pltpu.VMEM((1, cols), jnp.int32),
            dma, dma((chunks,)), dma((4,)),
            dma((line, subs)), dma((2, line)),
            dma((line,)), dma((line,)),
            dma((line,)), dma((line,)),
            dma((nz,)), dma((line,)),
            dma, dma, pltpu.SemaphoreType.REGULAR,
        ],
        compiler_params=pltpu.CompilerParams(
            collective_id=0, has_side_effects=True, vmem_limit_bytes=63 * 1024 * 1024),
    )(amplitudes, integrals, residual, ij, cd.reshape(1, depth), ab.reshape(1, cols))


def solution(mesh):
    line = mesh.shape["ab"] // CORES
    planes = mesh.shape["cd"] // NX
    ny = min(NY, planes)
    nz = planes // ny

    placed = (P("ab", "cd"), P("cd", "ab"), P("cd", "ab"), P("ab"), P("cd"), P("ab"))
    return jax.shard_map(functools.partial(ladder, line, ny, nz), mesh=mesh, in_specs=placed,
                         out_specs=P("cd", "ab"), check_vma=False)
```

```python
import functools

import jax
import jax.numpy as jnp
from jax import lax
from jax.experimental import pallas as pl
from jax.experimental.pallas import tpu as pltpu
from jax.sharding import PartitionSpec as P

MESH = pl.DeviceIdType.MESH
CORES = 2
NX = 4
NY = 4
SUB = 8
CUTS = 2
PARTS = 4
FIRST = 4


def kernel(line, ny, nz, t_hbm, v_hbm, res_hbm, ij_hbm, cd_hbm, ab_hbm, out_ref,
           tbuf, vraw, vhi, vlo, acc, sbuf, xr, ys, yr, zs, zr, keep, res, ij_ref, cd_ref, ab_ref,
           t_sem, v_sem, small_sem, line_recv, line_send, sib_recv, sib_send,
           x_recv, x_send, y_recv, y_send, z_recv, z_send, z_here):
    p, q = lax.axis_index("cd"), lax.axis_index("ab")
    x, y, h = p % NX, (p // NX) % ny, p // (NX * ny)
    core, i = q % CORES, q // CORES
    rows, depth = t_hbm.shape
    cols = v_hbm.shape[1]
    half = cols // 2
    subs = rows // SUB * CUTS
    width = depth // CUTS
    chunks = v_sem.shape[0]
    chunk = depth // chunks

    def plane(yy, xx):
        return (h * ny * NX + yy * NX + xx, q)

    sibling = (p, i * CORES + 1 - core)
    right, left = (p, q + CORES), (p, q - CORES)
    partner = ((p + ny * NX) % (nz * ny * NX), q)

    t_in = pltpu.make_async_copy(t_hbm, tbuf.at[q], t_sem)
    t_in.start()

    barrier = pltpu.get_barrier_semaphore()

    def greet(device):
        pl.semaphore_signal(barrier, inc=1, device_id=device, device_id_type=MESH)

    if nz > 1:
        pl.when(h == 0)(lambda: greet(partner))
    pl.when(i > 0)(lambda: greet(left))
    pl.when(i < line - 1)(lambda: greet(right))
    for d in range(1, NX):
        greet(plane(y, (x + d) % NX))
    for d in range(1, ny):
        greet(plane((y + d) % ny, x))
    greet(sibling)

    small = [pltpu.make_async_copy(a, b, small_sem.at[n])
             for n, (a, b) in enumerate(((ij_hbm, ij_ref), (cd_hbm, cd_ref), (ab_hbm, ab_ref), (res_hbm, res)))]
    for copy in small:
        copy.start()
    v_in = [pltpu.make_async_copy(v_hbm.at[pl.ds(c * chunk, chunk)], vraw.at[pl.ds(c * chunk, chunk)], v_sem.at[c])
            for c in range(chunks)]
    for copy in v_in:
        copy.start()

    small[0].wait()
    small[1].wait()
    t_in.wait()
    sub = lax.broadcasted_iota(jnp.int32, (SUB, 128), 0)
    for g in range(rows // SUB):
        label = jnp.zeros((SUB, 128), jnp.int32)
        for r in range(SUB):
            label = jnp.where(sub == r, ij_ref[g * SUB + r], label)
        for c in range(0, depth, 128):
            block = tbuf[q, g * SUB:(g + 1) * SUB, c:c + 128]
            tbuf[q, g * SUB:(g + 1) * SUB, c:c + 128] = jnp.where(label == cd_ref[:, c:c + 128], block, 0.0)

    others = 1 + (NX - 1) + (ny - 1) + (jnp.where(h > 0, 1, 0) if nz > 1 else 0)
    ends = jnp.where(i > 0, 1, 0) + jnp.where(i < line - 1, 1, 0)
    pl.semaphore_wait(barrier, others + ends)

    def remote(src, dst, send, recv, device):
        return pltpu.make_async_remote_copy(
            src_ref=src, dst_ref=dst, send_sem=send, recv_sem=recv, device_id=device, device_id_type=MESH)

    def piece(j, which, c):
        start = pl.multiple_of(c % CUTS * width, width)
        return tbuf.at[j * CORES + which, pl.ds(pl.multiple_of(c // CUTS * SUB, SUB), SUB), pl.ds(start, width)]

    m = line // 2
    held = subs - FIRST

    def behind(side):
        return jnp.where(side == 0, i, line - 1 - i)

    def number(side, b):
        return jnp.where(side == 0, b, line - 1 - b)

    def late(side):
        return (h > 0) & (side == 0)

    def near(side):
        return jnp.where(late(side), jnp.maximum(behind(side) - m, 0), 0)

    def arrival(side, n):
        k = near(side)
        ahead = k * FIRST
        r = n - ahead
        far = (k > 0) & (r >= 0) & (r < m * subs)
        e = jnp.where((k > 0) & (r >= m * subs), n - m * subs, n)
        b = jnp.where(far, m - 1 - r // subs, behind(side) - 1 - e // subs)
        c = jnp.where(far, r % subs, e % subs)
        return number(side, b), c, (k == 0) | (r < -held) | (r >= 0)

    def keeps(side):
        return late(side) & (behind(side) >= m) & (behind(side) < line - 1)

    def kept(side, n):
        k = near(side)
        r = jnp.where(k > 0, k * FIRST - held + n, n)
        return (number(side, jnp.where(k > 0, behind(side) - 1 - r // subs, m)),
                jnp.where(k > 0, r % subs, FIRST + n))

    def withheld(side):
        return keeps(side) & (near(side) == 0)

    def line_copy(j, c, way):
        part = piece(j, core, c)
        return remote(part, part, line_send.at[way, j], line_recv.at[j, c], right if way == 0 else left)

    def sib_copy(j, c):
        part = piece(j, core, c)
        return remote(part, part, sib_send.at[j], sib_recv.at[j], sibling)

    def forward(j, c, way):
        pl.when(i < line - 1 if way == 0 else i > 0)(lambda: line_copy(j, c, way).start())

    def forward_done(j):
        mine = tbuf.at[j * CORES + core]
        for way, there in ((0, (j <= i) & (i < line - 1)), (1, (j >= i) & (i > 0))):
            @pl.when(there & ((j != i) | jnp.logical_not(withheld(way))))
            def _():
                remote(mine, mine, line_send.at[way, j], line_recv.at[j, 0], sibling).wait_send()
        remote(mine, mine, sib_send.at[j], sib_recv.at[j], sibling).wait_send()

    def sib_wait(j):
        other = tbuf.at[j * CORES + 1 - core]
        remote(other, other, sib_send.at[j], sib_recv.at[j], sibling).wait_recv()

    for c in range(subs):
        for way in range(2):
            if c < FIRST:
                forward(i, c, way)
            else:
                pl.when(jnp.logical_not(withheld(way)))(lambda: forward(i, c, way))
    for c in range(subs):
        sib_copy(i, c).start()

    if nz > 1:
        @pl.when(h > 0)
        def _():
            pl.semaphore_signal(z_here, inc=1, device_id=partner, device_id_type=MESH)

    small[2].wait()
    for c in range(chunks):
        v_in[c].wait()

        @pl.loop(0, chunk // 128)
        def _(b):
            start = pl.multiple_of(c * chunk + b * 128, 128)
            label = jnp.broadcast_to(cd_ref[:, pl.ds(start, 128)], (128, 128)).T
            for l in range(0, cols, 128):
                v = jnp.where(label == ab_ref[:, l:l + 128], vraw[pl.ds(start, 128), l:l + 128], 0.0)
                hi = v.astype(jnp.bfloat16)
                vhi[pl.ds(start, 128), l:l + 128] = hi
                vlo[pl.ds(start, 128), l:l + 128] = (v - hi.astype(jnp.float32)).astype(jnp.bfloat16)

    def x_copy(j, d):
        k = (x + d) % NX
        return remote(sbuf.at[j, k], xr.at[j, d - 1], x_send.at[j], x_recv.at[j], plane(y, k))

    def y_copy(j):
        d = (j - y + ny) % ny
        return remote(ys.at[j], yr.at[j // ny, d - 1], y_send.at[j], y_recv.at[j // ny], plane(j % ny, x))

    def z_copy():
        return remote(zs, zr, z_send, z_recv, partner)

    low = lax.broadcasted_iota(jnp.int32, (8, half), 0) < 4

    def product(blocks, start, size):
        t = jnp.concatenate([tbuf[pl.ds(j * CORES, CORES), :, pl.ds(start, size)].reshape(CORES * rows, size)
                             for j in blocks], axis=0)
        n = t.shape[0]
        hi = t.astype(jnp.bfloat16)
        lo = (t - hi.astype(jnp.float32)).astype(jnp.bfloat16)
        a = jnp.dot(jnp.concatenate([hi, lo], axis=0), vhi[pl.ds(start, size)], preferred_element_type=jnp.float32)
        b = jnp.dot(hi, vlo[pl.ds(start, size)], preferred_element_type=jnp.float32)
        return a[:n] + a[n:] + b

    def hand_out(j, n):
        for k in range(NX):
            base = (k // 2) * rows
            middle = acc[n, base + 8:base + 16]
            turned = pltpu.roll(middle, 4, 0)
            if k % 2 == 0:
                full = acc[n, base:base + 8]
                rest = jnp.where(low, middle[:, :half], turned[:, half:])
            else:
                full = acc[n, base + 16:base + 24]
                rest = jnp.where(low, turned[:, :half], middle[:, half:])
            sbuf[j, k, :, :cols] = full
            sbuf[j, k, :, cols:] = rest
        for d in range(1, NX):
            x_copy(j, d).start()

    def reduce_x(j):
        remote(xr.at[j], xr.at[j], x_send.at[j], x_recv.at[j], sibling).wait_recv()
        mine = sbuf[j, x]
        for d in range(1, NX):
            mine = mine + xr[j, d - 1]
        ys[j] = mine
        pl.when(j % ny != y)(lambda: y_copy(j).start())

    def reduce_y(j):
        @pl.when(j % ny == y)
        def _():
            hh = j // ny
            mine = ys[j]
            if ny > 1:
                remote(yr.at[hh], yr.at[hh], y_send.at[j], y_recv.at[hh], sibling).wait_recv()
                for d in range(1, ny):
                    mine = mine + yr[hh, d - 1]

            @pl.when(hh == h)
            def _():
                keep[...] = mine

            @pl.when(hh != h)
            def _():
                zs[...] = mine
                pl.when(h == 0)(lambda: pl.semaphore_wait(z_here, 1))
                z_copy().start()

    def let_go(j):
        forward_done(j)
        sent = sbuf.at[j, pl.ds(0, NX - 1)]
        remote(sent, sent, x_send.at[j], x_recv.at[j], sibling).wait_send()
        pl.when(j % ny != y)(lambda: y_copy(j).wait_send())

    def complete(side, step):
        u, k = behind(side), near(side)
        early, lead = k * FIRST // subs, (k * FIRST + subs - 1) // subs
        far = (k > 0) & (step > early)
        b = jnp.where(far, m + lead, u) - step
        there = (step > 0) & (b >= jnp.where(k > 0, 1, 0)) & (jnp.logical_not(far) | (b < m))
        return jnp.where(step == 0, side == 0, there), jnp.where(step == 0, i, number(side, b))

    def at(step, act):
        @pl.loop(0, 2)
        def _(side):
            there, j = complete(side, step)
            pl.when(there)(lambda: act(j))

    def whole(j):
        sib_wait(j)
        acc[2] = product([j], 0, depth)
        hand_out(j, 2)

    def both(step, part):
        (there, j), (there_too, j_too) = complete(0, step), complete(1, step)

        @pl.when(there | there_too)
        def _():
            @pl.when(part == 0)
            def _():
                pl.when(there)(lambda: sib_wait(j))
                pl.when(there_too)(lambda: sib_wait(j_too))

            size = depth // PARTS
            start = pl.multiple_of(part * size, size)
            term = product([jnp.where(there, j, j_too), jnp.where(there_too, j_too, j)], start, size)
            term = term.reshape(2, CORES * rows, cols)

            @pl.when(part == 0)
            def _():
                acc[:2] = term

            @pl.when(part > 0)
            def _():
                acc[:2] += term

            @pl.when(part == PARTS - 1)
            def _():
                pl.when(there)(lambda: hand_out(j, 0))
                pl.when(there_too)(lambda: hand_out(j_too, 1))

    u, k = behind(0), near(0)
    last_far, rest = 0, m

    end = (i == 0) | (i == line - 1)

    @pl.loop(0, line + 2)
    def _(step):
        @pl.loop(0, subs)
        def _(c):
            for side in range(2):
                @pl.when((step > 0) & (step <= behind(side)))
                def _():
                    n = (step - 1) * subs + c
                    j, number_in_block, on = arrival(side, n)
                    line_copy(j, number_in_block, side).wait_recv()
                    pl.when(on)(lambda: forward(j, number_in_block, side))

                    @pl.when(keeps(side) & (n == near(side) * FIRST + m * subs - 1))
                    def _():
                        for e in range(held):
                            forward(*kept(side, e), side)

                    sib_copy(j, number_in_block).start()

            pl.when((k > 0) & ((step - 1) * subs + c == k * FIRST + m * subs - 1))(lambda: whole(last_far))

            @pl.when(jnp.logical_not(end) & (c < PARTS))
            def _():
                both(step - 1, c)

        pl.when(end)(lambda: at(step, whole))
        done = jnp.where(end, step, step - 1)
        final = jnp.where(end, u - 1, u)

        @pl.when((k == 0) | (step <= final))
        def _():
            at(done - 1, reduce_x)
            at(done - 2, reduce_y)

        @pl.when((k > 0) & (step == final))
        def _():
            pl.when(jnp.logical_not(end))(lambda: at(done, reduce_x))
            reduce_x(last_far)
            at(done - 1, reduce_y)
            pl.when(jnp.logical_not(end))(lambda: at(done, reduce_y))

        @pl.when((k > 0) & (step == u))
        def _():
            whole(rest)
            reduce_y(last_far)
            reduce_x(rest)
            reduce_y(rest)
            let_go(last_far)
            let_go(rest)

        at(done - 2, let_go)

    small[3].wait()
    if nz > 1:
        z_copy().wait_recv()
    mine = keep[...]
    if nz > 1:
        mine = mine + zr[...]
    full, rest = mine[:, :cols], mine[:, cols:]
    turned = pltpu.roll(rest, 4, 0)

    @pl.when(x % 2 == 0)
    def _():
        out_ref[:8] = full + res[:8]
        out_ref[8:12, :half] = rest[:4] + res[8:12, :half]
        out_ref[8:12, half:] = turned[:4] + res[8:12, half:]

    @pl.when(x % 2 == 1)
    def _():
        out_ref[:4, :half] = rest[:4] + res[:4, :half]
        out_ref[:4, half:] = turned[:4] + res[:4, half:]
        out_ref[4:12] = full + res[4:12]

    if nz > 1:
        z_copy().wait_send()
    for way in range(2):
        @pl.when(withheld(way))
        def _():
            mine = tbuf.at[i * CORES + core]
            remote(mine, mine, line_send.at[way, i], line_recv.at[i, 0], sibling).wait_send()


def ladder(line, ny, nz, amplitudes, integrals, residual, ij, cd, ab):
    rows, depth = amplitudes.shape
    cols = integrals.shape[1]
    subs = rows // SUB * CUTS
    piece = (8, cols + cols // 2)
    dma = pltpu.SemaphoreType.DMA
    chunks = min(4, depth // 128)
    return pl.pallas_call(
        functools.partial(kernel, line, ny, nz),
        out_shape=jax.ShapeDtypeStruct((rows // 2, cols), jnp.float32),
        in_specs=[pl.BlockSpec(memory_space=pltpu.HBM)] * 6,
        out_specs=pl.BlockSpec(memory_space=pltpu.VMEM),
        scratch_shapes=[
            pltpu.VMEM((line * CORES, rows, depth), jnp.float32),
            pltpu.VMEM((depth, cols), jnp.float32),
            pltpu.VMEM((depth, cols), jnp.bfloat16),
            pltpu.VMEM((depth, cols), jnp.bfloat16),
            pltpu.VMEM((3, CORES * rows, cols), jnp.float32),
            pltpu.VMEM((line, NX) + piece, jnp.float32),
            pltpu.VMEM((line, NX - 1) + piece, jnp.float32),
            pltpu.VMEM((line,) + piece, jnp.float32),
            pltpu.VMEM((nz, max(1, ny - 1)) + piece, jnp.float32),
            pltpu.VMEM(piece, jnp.float32),
            pltpu.VMEM(piece, jnp.float32),
            pltpu.VMEM(piece, jnp.float32),
            pltpu.VMEM((rows // 2, cols), jnp.float32),
            pltpu.SMEM((rows,), jnp.int32),
            pltpu.VMEM((1, depth), jnp.int32),
            pltpu.VMEM((1, cols), jnp.int32),
            dma, dma((chunks,)), dma((4,)),
            dma((line, subs)), dma((2, line)),
            dma((line,)), dma((line,)),
            dma((line,)), dma((line,)),
            dma((nz,)), dma((line,)),
            dma, dma, pltpu.SemaphoreType.REGULAR,
        ],
        compiler_params=pltpu.CompilerParams(
            collective_id=0, has_side_effects=True, vmem_limit_bytes=63 * 1024 * 1024),
    )(amplitudes, integrals, residual, ij, cd.reshape(1, depth), ab.reshape(1, cols))


def solution(mesh):
    line = mesh.shape["ab"] // CORES
    planes = mesh.shape["cd"] // NX
    ny = min(NY, planes)
    nz = planes // ny

    placed = (P("ab", "cd"), P("cd", "ab"), P("cd", "ab"), P("ab"), P("cd"), P("ab"))
    return jax.shard_map(functools.partial(ladder, line, ny, nz), mesh=mesh, in_specs=placed,
                         out_specs=P("cd", "ab"), check_vma=False)
```

```python
import functools

import jax
import jax.numpy as jnp
from jax import lax
from jax.experimental import pallas as pl
from jax.experimental.pallas import tpu as pltpu
from jax.sharding import PartitionSpec as P

MESH = pl.DeviceIdType.MESH
CORES = 2
NX = 4
NY = 4
SUB = 8
CUTS = 2
PARTS = 4
FIRST = 4


def kernel(line, ny, nz, t_hbm, v_hbm, res_hbm, ij_hbm, cd_hbm, ab_hbm, out_ref,
           tbuf, vraw, vhi, vlo, acc, sbuf, xr, ys, yr, zs, zr, keep, res, ij_ref, cd_ref, ab_ref,
           t_sem, v_sem, small_sem, line_recv, line_send, sib_recv, sib_send,
           x_recv, x_send, y_recv, y_send, z_recv, z_send, z_here):
    p, q = lax.axis_index("cd"), lax.axis_index("ab")
    x, y, h = p % NX, (p // NX) % ny, p // (NX * ny)
    core, i = q % CORES, q // CORES
    rows, depth = t_hbm.shape
    cols = v_hbm.shape[1]
    half = cols // 2
    subs = rows // SUB * CUTS
    width = depth // CUTS
    chunks = v_sem.shape[0]
    chunk = depth // chunks

    def plane(yy, xx):
        return (h * ny * NX + yy * NX + xx, q)

    sibling = (p, i * CORES + 1 - core)
    right, left = (p, q + CORES), (p, q - CORES)
    partner = ((p + ny * NX) % (nz * ny * NX), q)

    t_in = pltpu.make_async_copy(t_hbm, tbuf.at[q], t_sem)
    t_in.start()

    barrier = pltpu.get_barrier_semaphore()

    def greet(device):
        pl.semaphore_signal(barrier, inc=1, device_id=device, device_id_type=MESH)

    if nz > 1:
        pl.when(h == 0)(lambda: greet(partner))
    pl.when(i > 0)(lambda: greet(left))
    pl.when(i < line - 1)(lambda: greet(right))
    for d in range(1, NX):
        greet(plane(y, (x + d) % NX))
    for d in range(1, ny):
        greet(plane((y + d) % ny, x))
    greet(sibling)

    small = [pltpu.make_async_copy(a, b, small_sem.at[n])
             for n, (a, b) in enumerate(((ij_hbm, ij_ref), (cd_hbm, cd_ref), (ab_hbm, ab_ref), (res_hbm, res)))]
    for copy in small:
        copy.start()
    v_in = [pltpu.make_async_copy(v_hbm.at[pl.ds(c * chunk, chunk)], vraw.at[pl.ds(c * chunk, chunk)], v_sem.at[c])
            for c in range(chunks)]
    for copy in v_in:
        copy.start()

    small[0].wait()
    small[1].wait()
    t_in.wait()
    sub = lax.broadcasted_iota(jnp.int32, (SUB, 128), 0)
    for g in range(rows // SUB):
        label = jnp.zeros((SUB, 128), jnp.int32)
        for r in range(SUB):
            label = jnp.where(sub == r, ij_ref[g * SUB + r], label)
        for c in range(0, depth, 128):
            block = tbuf[q, g * SUB:(g + 1) * SUB, c:c + 128]
            tbuf[q, g * SUB:(g + 1) * SUB, c:c + 128] = jnp.where(label == cd_ref[:, c:c + 128], block, 0.0)

    others = 1 + (NX - 1) + (ny - 1) + (jnp.where(h > 0, 1, 0) if nz > 1 else 0)
    ends = jnp.where(i > 0, 1, 0) + jnp.where(i < line - 1, 1, 0)
    pl.semaphore_wait(barrier, others + ends)

    def remote(src, dst, send, recv, device):
        return pltpu.make_async_remote_copy(
            src_ref=src, dst_ref=dst, send_sem=send, recv_sem=recv, device_id=device, device_id_type=MESH)

    def piece(j, which, c):
        start = pl.multiple_of(c % CUTS * width, width)
        return tbuf.at[j * CORES + which, pl.ds(pl.multiple_of(c // CUTS * SUB, SUB), SUB), pl.ds(start, width)]

    m = line // 2
    held = subs - FIRST

    def behind(side):
        return jnp.where(side == 0, i, line - 1 - i)

    def number(side, b):
        return jnp.where(side == 0, b, line - 1 - b)

    def late(side):
        return (h > 0) & (side == 0)

    def near(side):
        return jnp.where(late(side), jnp.maximum(behind(side) - m, 0), 0)

    def arrival(side, n):
        k = near(side)
        ahead = k * FIRST
        r = n - ahead
        far = (k > 0) & (r >= 0) & (r < m * subs)
        e = jnp.where((k > 0) & (r >= m * subs), n - m * subs, n)
        b = jnp.where(far, m - 1 - r // subs, behind(side) - 1 - e // subs)
        c = jnp.where(far, r % subs, e % subs)
        return number(side, b), c, (k == 0) | (r < -held) | (r >= 0)

    def keeps(side):
        return late(side) & (behind(side) >= m) & (behind(side) < line - 1)

    def kept(side, n):
        k = near(side)
        r = jnp.where(k > 0, k * FIRST - held + n, n)
        return (number(side, jnp.where(k > 0, behind(side) - 1 - r // subs, m)),
                jnp.where(k > 0, r % subs, FIRST + n))

    def withheld(side):
        return keeps(side) & (near(side) == 0)

    def line_copy(j, c, way):
        part = piece(j, core, c)
        return remote(part, part, line_send.at[way, j], line_recv.at[j, c], right if way == 0 else left)

    def sib_copy(j, c):
        part = piece(j, core, c)
        return remote(part, part, sib_send.at[j], sib_recv.at[j], sibling)

    def forward(j, c, way):
        pl.when(i < line - 1 if way == 0 else i > 0)(lambda: line_copy(j, c, way).start())

    def forward_done(j):
        mine = tbuf.at[j * CORES + core]
        for way, there in ((0, (j <= i) & (i < line - 1)), (1, (j >= i) & (i > 0))):
            @pl.when(there & ((j != i) | jnp.logical_not(withheld(way))))
            def _():
                remote(mine, mine, line_send.at[way, j], line_recv.at[j, 0], sibling).wait_send()
        remote(mine, mine, sib_send.at[j], sib_recv.at[j], sibling).wait_send()

    def sib_wait(j):
        other = tbuf.at[j * CORES + 1 - core]
        remote(other, other, sib_send.at[j], sib_recv.at[j], sibling).wait_recv()

    for c in range(subs):
        for way in range(2):
            if c < FIRST:
                forward(i, c, way)
            else:
                pl.when(jnp.logical_not(withheld(way)))(lambda: forward(i, c, way))
    for c in range(subs):
        sib_copy(i, c).start()

    if nz > 1:
        @pl.when(h > 0)
        def _():
            pl.semaphore_signal(z_here, inc=1, device_id=partner, device_id_type=MESH)

    small[2].wait()
    for c in range(chunks):
        v_in[c].wait()

        @pl.loop(0, chunk // 128)
        def _(b):
            start = pl.multiple_of(c * chunk + b * 128, 128)
            label = jnp.broadcast_to(cd_ref[:, pl.ds(start, 128)], (128, 128)).T
            for l in range(0, cols, 128):
                v = jnp.where(label == ab_ref[:, l:l + 128], vraw[pl.ds(start, 128), l:l + 128], 0.0)
                hi = v.astype(jnp.bfloat16)
                vhi[pl.ds(start, 128), l:l + 128] = hi
                vlo[pl.ds(start, 128), l:l + 128] = (v - hi.astype(jnp.float32)).astype(jnp.bfloat16)

    def x_copy(j, d):
        k = (x + d) % NX
        return remote(sbuf.at[j, k], xr.at[j, d - 1], x_send.at[j], x_recv.at[j], plane(y, k))

    def y_copy(j):
        d = (j - y + ny) % ny
        return remote(ys.at[j], yr.at[j // ny, d - 1], y_send.at[j], y_recv.at[j // ny], plane(j % ny, x))

    def z_copy():
        return remote(zs, zr, z_send, z_recv, partner)

    low = lax.broadcasted_iota(jnp.int32, (8, half), 0) < 4

    def product(blocks, start, size):
        t = jnp.concatenate([tbuf[pl.ds(j * CORES, CORES), :, pl.ds(start, size)].reshape(CORES * rows, size)
                             for j in blocks], axis=0)
        n = t.shape[0]
        hi = t.astype(jnp.bfloat16)
        lo = (t - hi.astype(jnp.float32)).astype(jnp.bfloat16)
        a = jnp.dot(jnp.concatenate([hi, lo], axis=0), vhi[pl.ds(start, size)], preferred_element_type=jnp.float32)
        b = jnp.dot(hi, vlo[pl.ds(start, size)], preferred_element_type=jnp.float32)
        return a[:n] + a[n:] + b

    def hand_out(j, n):
        for k in range(NX):
            base = (k // 2) * rows
            middle = acc[n, base + 8:base + 16]
            turned = pltpu.roll(middle, 4, 0)
            if k % 2 == 0:
                full = acc[n, base:base + 8]
                rest = jnp.where(low, middle[:, :half], turned[:, half:])
            else:
                full = acc[n, base + 16:base + 24]
                rest = jnp.where(low, turned[:, :half], middle[:, half:])
            sbuf[j, k, :, :cols] = full
            sbuf[j, k, :, cols:] = rest
        for d in range(1, NX):
            x_copy(j, d).start()

    def reduce_x(j):
        remote(xr.at[j], xr.at[j], x_send.at[j], x_recv.at[j], sibling).wait_recv()
        mine = sbuf[j, x]
        for d in range(1, NX):
            mine = mine + xr[j, d - 1]
        ys[j] = mine
        pl.when(j % ny != y)(lambda: y_copy(j).start())

    def send_z():
        pl.when(h == 0)(lambda: pl.semaphore_wait(z_here, 1))
        z_copy().start()

    patient = ((h > 0) & (i <= m)) | ((h == 0) & (i == line - 1)) if nz > 1 else False
    halfway = patient & (i < 2)

    def reduce_y(j):
        @pl.when(j % ny == y)
        def _():
            hh = j // ny
            mine = ys[j]
            if ny > 1:
                remote(yr.at[hh], yr.at[hh], y_send.at[j], y_recv.at[hh], sibling).wait_recv()
                for d in range(1, ny):
                    mine = mine + yr[hh, d - 1]

            @pl.when(hh == h)
            def _():
                keep[...] = mine

            @pl.when(hh != h)
            def _():
                zs[...] = mine
                pl.when(jnp.logical_not(patient))(send_z)

    def let_go(j):
        forward_done(j)
        sent = sbuf.at[j, pl.ds(0, NX - 1)]
        remote(sent, sent, x_send.at[j], x_recv.at[j], sibling).wait_send()
        pl.when(j % ny != y)(lambda: y_copy(j).wait_send())

    def complete(side, step):
        u, k = behind(side), near(side)
        early, lead = k * FIRST // subs, (k * FIRST + subs - 1) // subs
        far = (k > 0) & (step > early)
        b = jnp.where(far, m + lead, u) - step
        there = (step > 0) & (b >= jnp.where(k > 0, 1, 0)) & (jnp.logical_not(far) | (b < m))
        return jnp.where(step == 0, side == 0, there), jnp.where(step == 0, i, number(side, b))

    def at(step, act):
        @pl.loop(0, 2)
        def _(side):
            there, j = complete(side, step)
            pl.when(there)(lambda: act(j))

    def whole(j):
        sib_wait(j)
        acc[2] = product([j], 0, depth)
        hand_out(j, 2)

    def both(step, part):
        (there, j), (there_too, j_too) = complete(0, step), complete(1, step)

        @pl.when(there | there_too)
        def _():
            @pl.when(part == 0)
            def _():
                pl.when(there)(lambda: sib_wait(j))
                pl.when(there_too)(lambda: sib_wait(j_too))

            size = depth // PARTS
            start = pl.multiple_of(part * size, size)
            term = product([jnp.where(there, j, j_too), jnp.where(there_too, j_too, j)], start, size)
            term = term.reshape(2, CORES * rows, cols)

            @pl.when(part == 0)
            def _():
                acc[:2] = term

            @pl.when(part > 0)
            def _():
                acc[:2] += term

            @pl.when(part == PARTS - 1)
            def _():
                pl.when(there)(lambda: hand_out(j, 0))
                pl.when(there_too)(lambda: hand_out(j_too, 1))

    u, k = behind(0), near(0)
    last_far, rest = 0, m

    end = (i == 0) | (i == line - 1)

    @pl.loop(0, line + 2)
    def _(step):
        @pl.loop(0, subs)
        def _(c):
            for side in range(2):
                @pl.when((step > 0) & (step <= behind(side)))
                def _():
                    n = (step - 1) * subs + c
                    j, number_in_block, on = arrival(side, n)
                    line_copy(j, number_in_block, side).wait_recv()
                    pl.when(on)(lambda: forward(j, number_in_block, side))

                    @pl.when(keeps(side) & (n == near(side) * FIRST + m * subs - 1))
                    def _():
                        for e in range(held):
                            forward(*kept(side, e), side)

                    sib_copy(j, number_in_block).start()

            pl.when((k > 0) & ((step - 1) * subs + c == k * FIRST + m * subs - 1))(lambda: whole(last_far))

            @pl.when(jnp.logical_not(end) & (c < PARTS))
            def _():
                both(step - 1, c)

        pl.when(end)(lambda: at(step, whole))
        done = jnp.where(end, step, step - 1)
        final = jnp.where(end, u - 1, u)

        @pl.when((k == 0) | (step <= final))
        def _():
            at(done - 1, reduce_x)
            at(done - 2, reduce_y)

        @pl.when((k > 0) & (step == final))
        def _():
            pl.when(jnp.logical_not(end))(lambda: at(done, reduce_x))
            reduce_x(last_far)
            at(done - 1, reduce_y)
            pl.when(jnp.logical_not(end))(lambda: at(done, reduce_y))

        @pl.when((k > 0) & (step == u))
        def _():
            whole(rest)
            reduce_y(last_far)
            reduce_x(rest)
            reduce_y(rest)
            let_go(last_far)
            let_go(rest)

        at(done - 2, let_go)
        pl.when(halfway & (step == line - 2))(send_z)

    small[3].wait()
    if nz > 1:
        pl.when(patient & jnp.logical_not(halfway))(send_z)
        z_copy().wait_recv()
    mine = keep[...]
    if nz > 1:
        mine = mine + zr[...]
    full, rest = mine[:, :cols], mine[:, cols:]
    turned = pltpu.roll(rest, 4, 0)

    @pl.when(x % 2 == 0)
    def _():
        out_ref[:8] = full + res[:8]
        out_ref[8:12, :half] = rest[:4] + res[8:12, :half]
        out_ref[8:12, half:] = turned[:4] + res[8:12, half:]

    @pl.when(x % 2 == 1)
    def _():
        out_ref[:4, :half] = rest[:4] + res[:4, :half]
        out_ref[:4, half:] = turned[:4] + res[:4, half:]
        out_ref[4:12] = full + res[4:12]

    if nz > 1:
        z_copy().wait_send()
    for way in range(2):
        @pl.when(withheld(way))
        def _():
            mine = tbuf.at[i * CORES + core]
            remote(mine, mine, line_send.at[way, i], line_recv.at[i, 0], sibling).wait_send()


def ladder(line, ny, nz, amplitudes, integrals, residual, ij, cd, ab):
    rows, depth = amplitudes.shape
    cols = integrals.shape[1]
    subs = rows // SUB * CUTS
    piece = (8, cols + cols // 2)
    dma = pltpu.SemaphoreType.DMA
    chunks = min(4, depth // 128)
    return pl.pallas_call(
        functools.partial(kernel, line, ny, nz),
        out_shape=jax.ShapeDtypeStruct((rows // 2, cols), jnp.float32),
        in_specs=[pl.BlockSpec(memory_space=pltpu.HBM)] * 6,
        out_specs=pl.BlockSpec(memory_space=pltpu.VMEM),
        scratch_shapes=[
            pltpu.VMEM((line * CORES, rows, depth), jnp.float32),
            pltpu.VMEM((depth, cols), jnp.float32),
            pltpu.VMEM((depth, cols), jnp.bfloat16),
            pltpu.VMEM((depth, cols), jnp.bfloat16),
            pltpu.VMEM((3, CORES * rows, cols), jnp.float32),
            pltpu.VMEM((line, NX) + piece, jnp.float32),
            pltpu.VMEM((line, NX - 1) + piece, jnp.float32),
            pltpu.VMEM((line,) + piece, jnp.float32),
            pltpu.VMEM((nz, max(1, ny - 1)) + piece, jnp.float32),
            pltpu.VMEM(piece, jnp.float32),
            pltpu.VMEM(piece, jnp.float32),
            pltpu.VMEM(piece, jnp.float32),
            pltpu.VMEM((rows // 2, cols), jnp.float32),
            pltpu.SMEM((rows,), jnp.int32),
            pltpu.VMEM((1, depth), jnp.int32),
            pltpu.VMEM((1, cols), jnp.int32),
            dma, dma((chunks,)), dma((4,)),
            dma((line, subs)), dma((2, line)),
            dma((line,)), dma((line,)),
            dma((line,)), dma((line,)),
            dma((nz,)), dma((line,)),
            dma, dma, pltpu.SemaphoreType.REGULAR,
        ],
        compiler_params=pltpu.CompilerParams(
            collective_id=0, has_side_effects=True, vmem_limit_bytes=63 * 1024 * 1024),
    )(amplitudes, integrals, residual, ij, cd.reshape(1, depth), ab.reshape(1, cols))


def solution(mesh):
    line = mesh.shape["ab"] // CORES
    planes = mesh.shape["cd"] // NX
    ny = min(NY, planes)
    nz = planes // ny

    placed = (P("ab", "cd"), P("cd", "ab"), P("cd", "ab"), P("ab"), P("cd"), P("ab"))
    return jax.shard_map(functools.partial(ladder, line, ny, nz), mesh=mesh, in_specs=placed,
                         out_specs=P("cd", "ab"), check_vma=False)
```

```python
import functools

import jax
import jax.numpy as jnp
from jax import lax
from jax.experimental import pallas as pl
from jax.experimental.pallas import tpu as pltpu
from jax.sharding import PartitionSpec as P

MESH = pl.DeviceIdType.MESH
CORES = 2
NX = 4
NY = 4
SUB = 8
CUTS = 2
PARTS = 4
FIRST = 4


def kernel(line, ny, nz, t_hbm, v_hbm, res_hbm, ij_hbm, cd_hbm, ab_hbm, out_ref,
           tbuf, vraw, vhi, vlo, acc, sbuf, xr, ys, yr, zs, zr, keep, res, ij_ref, cd_ref, ab_ref,
           t_sem, v_sem, small_sem, line_recv, line_send, sib_recv, sib_send,
           x_recv, x_send, y_recv, y_send, z_recv, z_send, z_here):
    p, q = lax.axis_index("cd"), lax.axis_index("ab")
    x, y, h = p % NX, (p // NX) % ny, p // (NX * ny)
    core, i = q % CORES, q // CORES
    rows, depth = t_hbm.shape
    cols = v_hbm.shape[1]
    half = cols // 2
    subs = rows // SUB * CUTS
    width = depth // CUTS
    chunks = v_sem.shape[0]
    chunk = depth // chunks

    def plane(yy, xx):
        return (h * ny * NX + yy * NX + xx, q)

    sibling = (p, i * CORES + 1 - core)
    right, left = (p, q + CORES), (p, q - CORES)
    partner = ((p + ny * NX) % (nz * ny * NX), q)

    t_in = pltpu.make_async_copy(t_hbm, tbuf.at[q], t_sem)
    t_in.start()

    barrier = pltpu.get_barrier_semaphore()

    def greet(device):
        pl.semaphore_signal(barrier, inc=1, device_id=device, device_id_type=MESH)

    if nz > 1:
        pl.when(h == 0)(lambda: greet(partner))
    pl.when(i > 0)(lambda: greet(left))
    pl.when(i < line - 1)(lambda: greet(right))
    for d in range(1, NX):
        greet(plane(y, (x + d) % NX))
    for d in range(1, ny):
        greet(plane((y + d) % ny, x))
    greet(sibling)

    small = [pltpu.make_async_copy(a, b, small_sem.at[n])
             for n, (a, b) in enumerate(((ij_hbm, ij_ref), (cd_hbm, cd_ref), (ab_hbm, ab_ref), (res_hbm, res)))]
    for copy in small:
        copy.start()
    v_in = [pltpu.make_async_copy(v_hbm.at[pl.ds(c * chunk, chunk)], vraw.at[pl.ds(c * chunk, chunk)], v_sem.at[c])
            for c in range(chunks)]
    for copy in v_in:
        copy.start()

    small[0].wait()
    small[1].wait()
    t_in.wait()
    sub = lax.broadcasted_iota(jnp.int32, (SUB, 128), 0)
    for g in range(rows // SUB):
        label = jnp.zeros((SUB, 128), jnp.int32)
        for r in range(SUB):
            label = jnp.where(sub == r, ij_ref[g * SUB + r], label)
        for c in range(0, depth, 128):
            block = tbuf[q, g * SUB:(g + 1) * SUB, c:c + 128]
            tbuf[q, g * SUB:(g + 1) * SUB, c:c + 128] = jnp.where(label == cd_ref[:, c:c + 128], block, 0.0)

    others = 1 + (NX - 1) + (ny - 1) + (jnp.where(h > 0, 1, 0) if nz > 1 else 0)
    ends = jnp.where(i > 0, 1, 0) + jnp.where(i < line - 1, 1, 0)
    pl.semaphore_wait(barrier, others + ends)

    def remote(src, dst, send, recv, device):
        return pltpu.make_async_remote_copy(
            src_ref=src, dst_ref=dst, send_sem=send, recv_sem=recv, device_id=device, device_id_type=MESH)

    def piece(j, which, c):
        start = pl.multiple_of(c % CUTS * width, width)
        return tbuf.at[j * CORES + which, pl.ds(pl.multiple_of(c // CUTS * SUB, SUB), SUB), pl.ds(start, width)]

    m = line // 2
    held = subs - FIRST

    def behind(side):
        return jnp.where(side == 0, i, line - 1 - i)

    def number(side, b):
        return jnp.where(side == 0, b, line - 1 - b)

    def late(side):
        return (h > 0) & (side == 0)

    def near(side):
        return jnp.where(late(side), jnp.maximum(behind(side) - m, 0), 0)

    def arrival(side, n):
        k = near(side)
        ahead = k * FIRST
        r = n - ahead
        far = (k > 0) & (r >= 0) & (r < m * subs)
        e = jnp.where((k > 0) & (r >= m * subs), n - m * subs, n)
        b = jnp.where(far, m - 1 - r // subs, behind(side) - 1 - e // subs)
        c = jnp.where(far, r % subs, e % subs)
        return number(side, b), c, (k == 0) | (r < -held) | (r >= 0)

    def keeps(side):
        return late(side) & (behind(side) >= m) & (behind(side) < line - 1)

    def kept(side, n):
        k = near(side)
        r = jnp.where(k > 0, k * FIRST - held + n, n)
        return (number(side, jnp.where(k > 0, behind(side) - 1 - r // subs, m)),
                jnp.where(k > 0, r % subs, FIRST + n))

    def withheld(side):
        return keeps(side) & (near(side) == 0)

    def line_copy(j, c, way):
        part = piece(j, core, c)
        return remote(part, part, line_send.at[way, j], line_recv.at[j, c], right if way == 0 else left)

    def sib_copy(j, g):
        part = tbuf.at[j * CORES + core, pl.ds(pl.multiple_of(g * SUB, SUB), SUB)]
        return remote(part, part, sib_send.at[j], sib_recv.at[j], sibling)

    def forward(j, c, way):
        pl.when(i < line - 1 if way == 0 else i > 0)(lambda: line_copy(j, c, way).start())

    def forward_done(j):
        mine = tbuf.at[j * CORES + core]
        for way, there in ((0, (j <= i) & (i < line - 1)), (1, (j >= i) & (i > 0))):
            @pl.when(there & ((j != i) | jnp.logical_not(withheld(way))))
            def _():
                remote(mine, mine, line_send.at[way, j], line_recv.at[j, 0], sibling).wait_send()
        remote(mine, mine, sib_send.at[j], sib_recv.at[j], sibling).wait_send()

    def sib_wait(j):
        other = tbuf.at[j * CORES + 1 - core]
        remote(other, other, sib_send.at[j], sib_recv.at[j], sibling).wait_recv()

    for c in range(subs):
        for way in range(2):
            if c < FIRST:
                forward(i, c, way)
            else:
                pl.when(jnp.logical_not(withheld(way)))(lambda: forward(i, c, way))
    for g in range(rows // SUB):
        sib_copy(i, g).start()

    if nz > 1:
        @pl.when(h > 0)
        def _():
            pl.semaphore_signal(z_here, inc=1, device_id=partner, device_id_type=MESH)

    small[2].wait()
    for c in range(chunks):
        v_in[c].wait()

        @pl.loop(0, chunk // 128)
        def _(b):
            start = pl.multiple_of(c * chunk + b * 128, 128)
            label = jnp.broadcast_to(cd_ref[:, pl.ds(start, 128)], (128, 128)).T
            for l in range(0, cols, 128):
                v = jnp.where(label == ab_ref[:, l:l + 128], vraw[pl.ds(start, 128), l:l + 128], 0.0)
                hi = v.astype(jnp.bfloat16)
                vhi[pl.ds(start, 128), l:l + 128] = hi
                vlo[pl.ds(start, 128), l:l + 128] = (v - hi.astype(jnp.float32)).astype(jnp.bfloat16)

    def x_copy(j, d):
        k = (x + d) % NX
        return remote(sbuf.at[j, k], xr.at[j, d - 1], x_send.at[j], x_recv.at[j], plane(y, k))

    def y_copy(j):
        d = (j - y + ny) % ny
        return remote(ys.at[j], yr.at[j // ny, d - 1], y_send.at[j], y_recv.at[j // ny], plane(j % ny, x))

    def z_copy():
        return remote(zs, zr, z_send, z_recv, partner)

    low = lax.broadcasted_iota(jnp.int32, (8, half), 0) < 4

    def product(blocks, start, size):
        t = jnp.concatenate([tbuf[pl.ds(j * CORES, CORES), :, pl.ds(start, size)].reshape(CORES * rows, size)
                             for j in blocks], axis=0)
        n = t.shape[0]
        hi = t.astype(jnp.bfloat16)
        lo = (t - hi.astype(jnp.float32)).astype(jnp.bfloat16)
        a = jnp.dot(jnp.concatenate([hi, lo], axis=0), vhi[pl.ds(start, size)], preferred_element_type=jnp.float32)
        b = jnp.dot(hi, vlo[pl.ds(start, size)], preferred_element_type=jnp.float32)
        return a[:n] + a[n:] + b

    def hand_out(j, n):
        for k in range(NX):
            base = (k // 2) * rows
            middle = acc[n, base + 8:base + 16]
            turned = pltpu.roll(middle, 4, 0)
            if k % 2 == 0:
                full = acc[n, base:base + 8]
                rest = jnp.where(low, middle[:, :half], turned[:, half:])
            else:
                full = acc[n, base + 16:base + 24]
                rest = jnp.where(low, turned[:, :half], middle[:, half:])
            sbuf[j, k, :, :cols] = full
            sbuf[j, k, :, cols:] = rest
        for d in sorted(range(1, NX), key=lambda d: -min(d, NX - d)):
            x_copy(j, d).start()

    def reduce_x(j):
        remote(xr.at[j], xr.at[j], x_send.at[j], x_recv.at[j], sibling).wait_recv()
        mine = sbuf[j, x]
        for d in range(1, NX):
            mine = mine + xr[j, d - 1]
        ys[j] = mine
        pl.when(j % ny != y)(lambda: y_copy(j).start())

    def send_z():
        pl.when(h == 0)(lambda: pl.semaphore_wait(z_here, 1))
        z_copy().start()

    patient = ((h > 0) & (i <= m)) | ((h == 0) & (i == line - 1)) if nz > 1 else False
    halfway = patient & (i < 2)

    def reduce_y(j):
        @pl.when(j % ny == y)
        def _():
            hh = j // ny
            mine = ys[j]
            if ny > 1:
                remote(yr.at[hh], yr.at[hh], y_send.at[j], y_recv.at[hh], sibling).wait_recv()
                for d in range(1, ny):
                    mine = mine + yr[hh, d - 1]

            @pl.when(hh == h)
            def _():
                keep[...] = mine

            @pl.when(hh != h)
            def _():
                zs[...] = mine
                pl.when(jnp.logical_not(patient))(send_z)

    def let_go(j):
        forward_done(j)
        sent = sbuf.at[j, pl.ds(0, NX - 1)]
        remote(sent, sent, x_send.at[j], x_recv.at[j], sibling).wait_send()
        pl.when(j % ny != y)(lambda: y_copy(j).wait_send())

    def complete(side, step):
        u, k = behind(side), near(side)
        early, lead = k * FIRST // subs, (k * FIRST + subs - 1) // subs
        far = (k > 0) & (step > early)
        b = jnp.where(far, m + lead, u) - step
        there = (step > 0) & (b >= jnp.where(k > 0, 1, 0)) & (jnp.logical_not(far) | (b < m))
        return jnp.where(step == 0, side == 0, there), jnp.where(step == 0, i, number(side, b))

    def at(step, act):
        @pl.loop(0, 2)
        def _(side):
            there, j = complete(side, step)
            pl.when(there)(lambda: act(j))

    def whole(j):
        sib_wait(j)
        acc[2] = product([j], 0, depth)
        hand_out(j, 2)

    def both(step, part):
        (there, j), (there_too, j_too) = complete(0, step), complete(1, step)

        @pl.when(there | there_too)
        def _():
            @pl.when(part == 0)
            def _():
                pl.when(there)(lambda: sib_wait(j))
                pl.when(there_too)(lambda: sib_wait(j_too))

            size = depth // PARTS
            start = pl.multiple_of(part * size, size)
            term = product([jnp.where(there, j, j_too), jnp.where(there_too, j_too, j)], start, size)
            term = term.reshape(2, CORES * rows, cols)

            @pl.when(part == 0)
            def _():
                acc[:2] = term

            @pl.when(part > 0)
            def _():
                acc[:2] += term

            @pl.when(part == PARTS - 1)
            def _():
                pl.when(there)(lambda: hand_out(j, 0))
                pl.when(there_too)(lambda: hand_out(j_too, 1))

    u, k = behind(0), near(0)
    last_far, rest = 0, m

    end = (i == 0) | (i == line - 1)

    @pl.loop(0, line + 2)
    def _(step):
        @pl.loop(0, subs)
        def _(c):
            for side in range(2):
                @pl.when((step > 0) & (step <= behind(side)))
                def _():
                    n = (step - 1) * subs + c
                    j, number_in_block, on = arrival(side, n)
                    line_copy(j, number_in_block, side).wait_recv()
                    pl.when(on)(lambda: forward(j, number_in_block, side))

                    @pl.when(keeps(side) & (n == near(side) * FIRST + m * subs - 1))
                    def _():
                        for e in range(held):
                            forward(*kept(side, e), side)

                    pl.when(number_in_block % CUTS == CUTS - 1)(
                        lambda: sib_copy(j, number_in_block // CUTS).start())

            pl.when((k > 0) & ((step - 1) * subs + c == k * FIRST + m * subs - 1))(lambda: whole(last_far))

            @pl.when(jnp.logical_not(end) & (c < PARTS))
            def _():
                both(step - 1, c)

        pl.when(end)(lambda: at(step, whole))
        done = jnp.where(end, step, step - 1)
        final = jnp.where(end, u - 1, u)

        @pl.when((k == 0) | (step <= final))
        def _():
            at(done - 1, reduce_x)
            at(done - 2, reduce_y)

        @pl.when((k > 0) & (step == final))
        def _():
            pl.when(jnp.logical_not(end))(lambda: at(done, reduce_x))
            reduce_x(last_far)
            at(done - 1, reduce_y)
            pl.when(jnp.logical_not(end))(lambda: at(done, reduce_y))

        @pl.when((k > 0) & (step == u))
        def _():
            whole(rest)
            reduce_y(last_far)
            reduce_x(rest)
            reduce_y(rest)
            let_go(last_far)
            let_go(rest)

        at(done - 2, let_go)
        pl.when(halfway & (step == line - 2))(send_z)

    small[3].wait()
    if nz > 1:
        pl.when(patient & jnp.logical_not(halfway))(send_z)
        z_copy().wait_recv()
    mine = keep[...]
    if nz > 1:
        mine = mine + zr[...]
    full, rest = mine[:, :cols], mine[:, cols:]
    turned = pltpu.roll(rest, 4, 0)

    @pl.when(x % 2 == 0)
    def _():
        out_ref[:8] = full + res[:8]
        out_ref[8:12, :half] = rest[:4] + res[8:12, :half]
        out_ref[8:12, half:] = turned[:4] + res[8:12, half:]

    @pl.when(x % 2 == 1)
    def _():
        out_ref[:4, :half] = rest[:4] + res[:4, :half]
        out_ref[:4, half:] = turned[:4] + res[:4, half:]
        out_ref[4:12] = full + res[4:12]

    if nz > 1:
        z_copy().wait_send()
    for way in range(2):
        @pl.when(withheld(way))
        def _():
            mine = tbuf.at[i * CORES + core]
            remote(mine, mine, line_send.at[way, i], line_recv.at[i, 0], sibling).wait_send()


def ladder(line, ny, nz, amplitudes, integrals, residual, ij, cd, ab):
    rows, depth = amplitudes.shape
    cols = integrals.shape[1]
    subs = rows // SUB * CUTS
    piece = (8, cols + cols // 2)
    dma = pltpu.SemaphoreType.DMA
    chunks = min(4, depth // 128)
    return pl.pallas_call(
        functools.partial(kernel, line, ny, nz),
        out_shape=jax.ShapeDtypeStruct((rows // 2, cols), jnp.float32),
        in_specs=[pl.BlockSpec(memory_space=pltpu.HBM)] * 6,
        out_specs=pl.BlockSpec(memory_space=pltpu.VMEM),
        scratch_shapes=[
            pltpu.VMEM((line * CORES, rows, depth), jnp.float32),
            pltpu.VMEM((depth, cols), jnp.float32),
            pltpu.VMEM((depth, cols), jnp.bfloat16),
            pltpu.VMEM((depth, cols), jnp.bfloat16),
            pltpu.VMEM((3, CORES * rows, cols), jnp.float32),
            pltpu.VMEM((line, NX) + piece, jnp.float32),
            pltpu.VMEM((line, NX - 1) + piece, jnp.float32),
            pltpu.VMEM((line,) + piece, jnp.float32),
            pltpu.VMEM((nz, max(1, ny - 1)) + piece, jnp.float32),
            pltpu.VMEM(piece, jnp.float32),
            pltpu.VMEM(piece, jnp.float32),
            pltpu.VMEM(piece, jnp.float32),
            pltpu.VMEM((rows // 2, cols), jnp.float32),
            pltpu.SMEM((rows,), jnp.int32),
            pltpu.VMEM((1, depth), jnp.int32),
            pltpu.VMEM((1, cols), jnp.int32),
            dma, dma((chunks,)), dma((4,)),
            dma((line, subs)), dma((2, line)),
            dma((line,)), dma((line,)),
            dma((line,)), dma((line,)),
            dma((nz,)), dma((line,)),
            dma, dma, pltpu.SemaphoreType.REGULAR,
        ],
        compiler_params=pltpu.CompilerParams(
            collective_id=0, has_side_effects=True, vmem_limit_bytes=63 * 1024 * 1024),
    )(amplitudes, integrals, residual, ij, cd.reshape(1, depth), ab.reshape(1, cols))


def solution(mesh):
    line = mesh.shape["ab"] // CORES
    planes = mesh.shape["cd"] // NX
    ny = min(NY, planes)
    nz = planes // ny

    placed = (P("ab", "cd"), P("cd", "ab"), P("cd", "ab"), P("ab"), P("cd"), P("ab"))
    return jax.shard_map(functools.partial(ladder, line, ny, nz), mesh=mesh, in_specs=placed,
                         out_specs=P("cd", "ab"), check_vma=False)
```

```python
import functools

import jax
import jax.numpy as jnp
from jax import lax
from jax.experimental import pallas as pl
from jax.experimental.pallas import tpu as pltpu
from jax.sharding import PartitionSpec as P

MESH = pl.DeviceIdType.MESH
CORES = 2
NX = 4
NY = 4
SUB = 8
CUTS = 2
PARTS = 4
FIRST = 4


def kernel(line, ny, nz, t_hbm, v_hbm, res_hbm, ij_hbm, cd_hbm, ab_hbm, out_ref,
           tbuf, vraw, vhi, vlo, acc, sbuf, xr, ys, yr, zs, zr, keep, res, ij_ref, cd_ref, ab_ref,
           t_sem, v_sem, small_sem, line_recv, line_send, sib_recv, sib_send,
           x_recv, x_send, y_recv, y_send, z_recv, z_send, z_here):
    p, q = lax.axis_index("cd"), lax.axis_index("ab")
    x, y, h = p % NX, (p // NX) % ny, p // (NX * ny)
    core, i = q % CORES, q // CORES
    rows, depth = t_hbm.shape
    cols = v_hbm.shape[1]
    half = cols // 2
    subs = rows // SUB * CUTS
    width = depth // CUTS
    chunks = v_sem.shape[0]
    chunk = depth // chunks

    def plane(yy, xx):
        return (h * ny * NX + yy * NX + xx, q)

    sibling = (p, i * CORES + 1 - core)
    right, left = (p, q + CORES), (p, q - CORES)
    partner = ((p + ny * NX) % (nz * ny * NX), q)

    t_in = pltpu.make_async_copy(t_hbm, tbuf.at[q], t_sem)
    t_in.start()

    barrier = pltpu.get_barrier_semaphore()

    def greet(device):
        pl.semaphore_signal(barrier, inc=1, device_id=device, device_id_type=MESH)

    if nz > 1:
        pl.when(h == 0)(lambda: greet(partner))
    pl.when(i > 0)(lambda: greet(left))
    pl.when(i < line - 1)(lambda: greet(right))
    for d in range(1, NX):
        greet(plane(y, (x + d) % NX))
    for d in range(1, ny):
        greet(plane((y + d) % ny, x))
    greet(sibling)

    small = [pltpu.make_async_copy(a, b, small_sem.at[n])
             for n, (a, b) in enumerate(((ij_hbm, ij_ref), (cd_hbm, cd_ref), (ab_hbm, ab_ref), (res_hbm, res)))]
    for copy in small:
        copy.start()
    v_in = [pltpu.make_async_copy(v_hbm.at[pl.ds(c * chunk, chunk)], vraw.at[pl.ds(c * chunk, chunk)], v_sem.at[c])
            for c in range(chunks)]
    for copy in v_in:
        copy.start()

    small[0].wait()
    small[1].wait()
    t_in.wait()
    sub = lax.broadcasted_iota(jnp.int32, (SUB, 128), 0)
    for g in range(rows // SUB):
        label = jnp.zeros((SUB, 128), jnp.int32)
        for r in range(SUB):
            label = jnp.where(sub == r, ij_ref[g * SUB + r], label)
        for c in range(0, depth, 128):
            block = tbuf[q, g * SUB:(g + 1) * SUB, c:c + 128]
            tbuf[q, g * SUB:(g + 1) * SUB, c:c + 128] = jnp.where(label == cd_ref[:, c:c + 128], block, 0.0)

    small[2].wait()

    def split(c):
        v_in[c].wait()

        @pl.loop(0, chunk // 128)
        def _(b):
            start = pl.multiple_of(c * chunk + b * 128, 128)
            label = jnp.broadcast_to(cd_ref[:, pl.ds(start, 128)], (128, 128)).T
            for l in range(0, cols, 128):
                v = jnp.where(label == ab_ref[:, l:l + 128], vraw[pl.ds(start, 128), l:l + 128], 0.0)
                hi = v.astype(jnp.bfloat16)
                vhi[pl.ds(start, 128), l:l + 128] = hi
                vlo[pl.ds(start, 128), l:l + 128] = (v - hi.astype(jnp.float32)).astype(jnp.bfloat16)

    split(0)

    others = 1 + (NX - 1) + (ny - 1) + (jnp.where(h > 0, 1, 0) if nz > 1 else 0)
    ends = jnp.where(i > 0, 1, 0) + jnp.where(i < line - 1, 1, 0)
    pl.semaphore_wait(barrier, others + ends)

    def remote(src, dst, send, recv, device):
        return pltpu.make_async_remote_copy(
            src_ref=src, dst_ref=dst, send_sem=send, recv_sem=recv, device_id=device, device_id_type=MESH)

    def piece(j, which, c):
        start = pl.multiple_of(c % CUTS * width, width)
        return tbuf.at[j * CORES + which, pl.ds(pl.multiple_of(c // CUTS * SUB, SUB), SUB), pl.ds(start, width)]

    m = line // 2
    held = subs - FIRST

    def behind(side):
        return jnp.where(side == 0, i, line - 1 - i)

    def number(side, b):
        return jnp.where(side == 0, b, line - 1 - b)

    def late(side):
        return (h > 0) & (side == 0)

    def near(side):
        return jnp.where(late(side), jnp.maximum(behind(side) - m, 0), 0)

    def arrival(side, n):
        k = near(side)
        ahead = k * FIRST
        r = n - ahead
        far = (k > 0) & (r >= 0) & (r < m * subs)
        e = jnp.where((k > 0) & (r >= m * subs), n - m * subs, n)
        b = jnp.where(far, m - 1 - r // subs, behind(side) - 1 - e // subs)
        c = jnp.where(far, r % subs, e % subs)
        return number(side, b), c, (k == 0) | (r < -held) | (r >= 0)

    def keeps(side):
        return late(side) & (behind(side) >= m) & (behind(side) < line - 1)

    def kept(side, n):
        k = near(side)
        r = jnp.where(k > 0, k * FIRST - held + n, n)
        return (number(side, jnp.where(k > 0, behind(side) - 1 - r // subs, m)),
                jnp.where(k > 0, r % subs, FIRST + n))

    def withheld(side):
        return keeps(side) & (near(side) == 0)

    def line_copy(j, c, way):
        part = piece(j, core, c)
        return remote(part, part, line_send.at[way, j], line_recv.at[j, c], right if way == 0 else left)

    def sib_copy(j, g):
        part = tbuf.at[j * CORES + core, pl.ds(pl.multiple_of(g * SUB, SUB), SUB)]
        return remote(part, part, sib_send.at[j], sib_recv.at[j], sibling)

    def forward(j, c, way):
        pl.when(i < line - 1 if way == 0 else i > 0)(lambda: line_copy(j, c, way).start())

    def forward_done(j):
        mine = tbuf.at[j * CORES + core]
        for way, there in ((0, (j <= i) & (i < line - 1)), (1, (j >= i) & (i > 0))):
            @pl.when(there & ((j != i) | jnp.logical_not(withheld(way))))
            def _():
                remote(mine, mine, line_send.at[way, j], line_recv.at[j, 0], sibling).wait_send()
        remote(mine, mine, sib_send.at[j], sib_recv.at[j], sibling).wait_send()

    def sib_wait(j):
        other = tbuf.at[j * CORES + 1 - core]
        remote(other, other, sib_send.at[j], sib_recv.at[j], sibling).wait_recv()

    for c in range(subs):
        for way in range(2):
            if c < FIRST:
                forward(i, c, way)
            else:
                pl.when(jnp.logical_not(withheld(way)))(lambda: forward(i, c, way))
    for g in range(rows // SUB):
        sib_copy(i, g).start()

    if nz > 1:
        @pl.when(h > 0)
        def _():
            pl.semaphore_signal(z_here, inc=1, device_id=partner, device_id_type=MESH)

    for c in range(1, chunks):
        split(c)

    def x_copy(j, d):
        k = (x + d) % NX
        return remote(sbuf.at[j, k], xr.at[j, d - 1], x_send.at[j], x_recv.at[j], plane(y, k))

    def y_copy(j):
        d = (j - y + ny) % ny
        return remote(ys.at[j], yr.at[j // ny, d - 1], y_send.at[j], y_recv.at[j // ny], plane(j % ny, x))

    def z_copy():
        return remote(zs, zr, z_send, z_recv, partner)

    low = lax.broadcasted_iota(jnp.int32, (8, half), 0) < 4

    def product(blocks, start, size):
        t = jnp.concatenate([tbuf[pl.ds(j * CORES, CORES), :, pl.ds(start, size)].reshape(CORES * rows, size)
                             for j in blocks], axis=0)
        n = t.shape[0]
        hi = t.astype(jnp.bfloat16)
        lo = (t - hi.astype(jnp.float32)).astype(jnp.bfloat16)
        a = jnp.dot(jnp.concatenate([hi, lo], axis=0), vhi[pl.ds(start, size)], preferred_element_type=jnp.float32)
        b = jnp.dot(hi, vlo[pl.ds(start, size)], preferred_element_type=jnp.float32)
        return a[:n] + a[n:] + b

    def hand_out(j, n):
        for k in range(NX):
            base = (k // 2) * rows
            middle = acc[n, base + 8:base + 16]
            turned = pltpu.roll(middle, 4, 0)
            if k % 2 == 0:
                full = acc[n, base:base + 8]
                rest = jnp.where(low, middle[:, :half], turned[:, half:])
            else:
                full = acc[n, base + 16:base + 24]
                rest = jnp.where(low, turned[:, :half], middle[:, half:])
            sbuf[j, k, :, :cols] = full
            sbuf[j, k, :, cols:] = rest
        for d in sorted(range(1, NX), key=lambda d: -min(d, NX - d)):
            x_copy(j, d).start()

    def reduce_x(j):
        remote(xr.at[j], xr.at[j], x_send.at[j], x_recv.at[j], sibling).wait_recv()
        mine = sbuf[j, x]
        for d in range(1, NX):
            mine = mine + xr[j, d - 1]
        ys[j] = mine
        pl.when(j % ny != y)(lambda: y_copy(j).start())

    def send_z():
        pl.when(h == 0)(lambda: pl.semaphore_wait(z_here, 1))
        z_copy().start()

    patient = ((h > 0) & (i <= m)) | ((h == 0) & (i == line - 1)) if nz > 1 else False
    halfway = patient & (i < 2)

    def reduce_y(j):
        @pl.when(j % ny == y)
        def _():
            hh = j // ny
            mine = ys[j]
            if ny > 1:
                remote(yr.at[hh], yr.at[hh], y_send.at[j], y_recv.at[hh], sibling).wait_recv()
                for d in range(1, ny):
                    mine = mine + yr[hh, d - 1]

            @pl.when(hh == h)
            def _():
                keep[...] = mine

            @pl.when(hh != h)
            def _():
                zs[...] = mine
                pl.when(jnp.logical_not(patient))(send_z)

    def let_go(j):
        forward_done(j)
        sent = sbuf.at[j, pl.ds(0, NX - 1)]
        remote(sent, sent, x_send.at[j], x_recv.at[j], sibling).wait_send()
        pl.when(j % ny != y)(lambda: y_copy(j).wait_send())

    def complete(side, step):
        u, k = behind(side), near(side)
        early, lead = k * FIRST // subs, (k * FIRST + subs - 1) // subs
        far = (k > 0) & (step > early)
        b = jnp.where(far, m + lead, u) - step
        there = (step > 0) & (b >= jnp.where(k > 0, 1, 0)) & (jnp.logical_not(far) | (b < m))
        return jnp.where(step == 0, side == 0, there), jnp.where(step == 0, i, number(side, b))

    def at(step, act):
        @pl.loop(0, 2)
        def _(side):
            there, j = complete(side, step)
            pl.when(there)(lambda: act(j))

    def whole(j):
        sib_wait(j)
        acc[2] = product([j], 0, depth)
        hand_out(j, 2)

    def both(step, part):
        (there, j), (there_too, j_too) = complete(0, step), complete(1, step)

        @pl.when(there | there_too)
        def _():
            @pl.when(part == 0)
            def _():
                pl.when(there)(lambda: sib_wait(j))
                pl.when(there_too)(lambda: sib_wait(j_too))

            size = depth // PARTS
            start = pl.multiple_of(part * size, size)
            term = product([jnp.where(there, j, j_too), jnp.where(there_too, j_too, j)], start, size)
            term = term.reshape(2, CORES * rows, cols)

            @pl.when(part == 0)
            def _():
                acc[:2] = term

            @pl.when(part > 0)
            def _():
                acc[:2] += term

            @pl.when(part == PARTS - 1)
            def _():
                pl.when(there)(lambda: hand_out(j, 0))
                pl.when(there_too)(lambda: hand_out(j_too, 1))

    u, k = behind(0), near(0)
    last_far, rest = 0, m

    end = (i == 0) | (i == line - 1)

    @pl.loop(0, line + 2)
    def _(step):
        @pl.loop(0, subs)
        def _(c):
            for side in range(2):
                @pl.when((step > 0) & (step <= behind(side)))
                def _():
                    n = (step - 1) * subs + c
                    j, number_in_block, on = arrival(side, n)
                    line_copy(j, number_in_block, side).wait_recv()
                    pl.when(on)(lambda: forward(j, number_in_block, side))

                    @pl.when(keeps(side) & (n == near(side) * FIRST + m * subs - 1))
                    def _():
                        for e in range(held):
                            forward(*kept(side, e), side)

                    pl.when(number_in_block % CUTS == CUTS - 1)(
                        lambda: sib_copy(j, number_in_block // CUTS).start())

            pl.when((k > 0) & ((step - 1) * subs + c == k * FIRST + m * subs - 1))(lambda: whole(last_far))

            @pl.when(jnp.logical_not(end) & (c < PARTS))
            def _():
                both(step - 1, c)

        pl.when(end)(lambda: at(step, whole))
        done = jnp.where(end, step, step - 1)
        final = jnp.where(end, u - 1, u)

        @pl.when((k == 0) | (step <= final))
        def _():
            at(done - 1, reduce_x)
            at(done - 2, reduce_y)

        @pl.when((k > 0) & (step == final))
        def _():
            pl.when(jnp.logical_not(end))(lambda: at(done, reduce_x))
            reduce_x(last_far)
            at(done - 1, reduce_y)
            pl.when(jnp.logical_not(end))(lambda: at(done, reduce_y))

        @pl.when((k > 0) & (step == u))
        def _():
            whole(rest)
            reduce_y(last_far)
            reduce_x(rest)
            reduce_y(rest)
            let_go(last_far)
            let_go(rest)

        at(done - 2, let_go)
        pl.when(halfway & (step == line - 2))(send_z)

    small[3].wait()
    if nz > 1:
        pl.when(patient & jnp.logical_not(halfway))(send_z)
        z_copy().wait_recv()
    mine = keep[...]
    if nz > 1:
        mine = mine + zr[...]
    full, rest = mine[:, :cols], mine[:, cols:]
    turned = pltpu.roll(rest, 4, 0)

    @pl.when(x % 2 == 0)
    def _():
        out_ref[:8] = full + res[:8]
        out_ref[8:12, :half] = rest[:4] + res[8:12, :half]
        out_ref[8:12, half:] = turned[:4] + res[8:12, half:]

    @pl.when(x % 2 == 1)
    def _():
        out_ref[:4, :half] = rest[:4] + res[:4, :half]
        out_ref[:4, half:] = turned[:4] + res[:4, half:]
        out_ref[4:12] = full + res[4:12]

    if nz > 1:
        z_copy().wait_send()
    for way in range(2):
        @pl.when(withheld(way))
        def _():
            mine = tbuf.at[i * CORES + core]
            remote(mine, mine, line_send.at[way, i], line_recv.at[i, 0], sibling).wait_send()


def ladder(line, ny, nz, amplitudes, integrals, residual, ij, cd, ab):
    rows, depth = amplitudes.shape
    cols = integrals.shape[1]
    subs = rows // SUB * CUTS
    piece = (8, cols + cols // 2)
    dma = pltpu.SemaphoreType.DMA
    chunks = min(4, depth // 128)
    return pl.pallas_call(
        functools.partial(kernel, line, ny, nz),
        out_shape=jax.ShapeDtypeStruct((rows // 2, cols), jnp.float32),
        in_specs=[pl.BlockSpec(memory_space=pltpu.HBM)] * 6,
        out_specs=pl.BlockSpec(memory_space=pltpu.VMEM),
        scratch_shapes=[
            pltpu.VMEM((line * CORES, rows, depth), jnp.float32),
            pltpu.VMEM((depth, cols), jnp.float32),
            pltpu.VMEM((depth, cols), jnp.bfloat16),
            pltpu.VMEM((depth, cols), jnp.bfloat16),
            pltpu.VMEM((3, CORES * rows, cols), jnp.float32),
            pltpu.VMEM((line, NX) + piece, jnp.float32),
            pltpu.VMEM((line, NX - 1) + piece, jnp.float32),
            pltpu.VMEM((line,) + piece, jnp.float32),
            pltpu.VMEM((nz, max(1, ny - 1)) + piece, jnp.float32),
            pltpu.VMEM(piece, jnp.float32),
            pltpu.VMEM(piece, jnp.float32),
            pltpu.VMEM(piece, jnp.float32),
            pltpu.VMEM((rows // 2, cols), jnp.float32),
            pltpu.SMEM((rows,), jnp.int32),
            pltpu.VMEM((1, depth), jnp.int32),
            pltpu.VMEM((1, cols), jnp.int32),
            dma, dma((chunks,)), dma((4,)),
            dma((line, subs)), dma((2, line)),
            dma((line,)), dma((line,)),
            dma((line,)), dma((line,)),
            dma((nz,)), dma((line,)),
            dma, dma, pltpu.SemaphoreType.REGULAR,
        ],
        compiler_params=pltpu.CompilerParams(
            collective_id=0, has_side_effects=True, vmem_limit_bytes=63 * 1024 * 1024),
    )(amplitudes, integrals, residual, ij, cd.reshape(1, depth), ab.reshape(1, cols))


def solution(mesh):
    line = mesh.shape["ab"] // CORES
    planes = mesh.shape["cd"] // NX
    ny = min(NY, planes)
    nz = planes // ny

    placed = (P("ab", "cd"), P("cd", "ab"), P("cd", "ab"), P("ab"), P("cd"), P("ab"))
    return jax.shard_map(functools.partial(ladder, line, ny, nz), mesh=mesh, in_specs=placed,
                         out_specs=P("cd", "ab"), check_vma=False)
```
